256 devices in a mesh: dp: 2 (over y_hi), row: 8 (over x, core), col: 16 (over y_lo, z).
Axes of the slice: x: 4, y: 4 (y_hi: 2, y_lo: 2; y = y_hi * 2 + y_lo), z: 8, core: 2. Of those that a mesh axis runs over, the one named last changes fastest.
Arguments:
- patches: bfloat16 [2, 2048, 1456], P('dp', 'col', 'row'), may hold values from -6 to 6
- queries: bfloat16 [2, 2048, 6144], P('dp', 'col', 'row'), may hold values from -6 to 6
- attn_keys: bfloat16 [2, 2048, 6144], P('dp', 'col', 'row'), may hold values from -6 to 6
- attn_values: bfloat16 [2, 2048, 6144], P('dp', 'col', 'row'), may hold values from -6 to 6
- out_weight: bfloat16 [6144, 12288], P('row', 'col'), may hold values from -0.15625 to 0.15625
- output_grad: bfloat16 [2, 2048, 12288], P('dp', 'row', 'col'), may hold values from -4 to 4
Outputs:
- query_grad: float32 [2, 2048, 6144], P('dp', 'col', 'row')
- key_grad: float32 [2, 2048, 6144], P('dp', 'col', 'row')
- value_grad: float32 [2, 2048, 6144], P('dp', 'col', 'row')
- out_weight_grad: float32 [6144, 12288], P('row', 'col')
- embed_weight_grad: float32 [1456, 12288], P('row', 'col')
The draws below stay inside these ranges and needn't reach their ends.
All inputs are finite; a program needn't handle non-finite values.
Results may differ from the reference program's by a relative error of at most 0.025.
Values may be sent and summed in bfloat16 or wider, within the bound.
A program may use at most 128 MiB of HBM per device.

```python
import jax
import jax.numpy as jnp
from jax import lax

D = 12288
H = 48
DH = 128
SEQ = 2048
BATCH = 2
HD = 6144
P_SIZE = 1456
DBLK = 768


def draw_queries(key, part):
    shape = (BATCH, SEQ, HD)
    return jnp.clip(0.5 * jax.random.normal(jax.random.fold_in(key, 1), shape, jnp.float32), -6.0, 6.0).astype(jnp.bfloat16)


def draw_attn_keys(key, part):
    shape = (BATCH, SEQ, HD)
    return jnp.clip(0.5 * jax.random.normal(jax.random.fold_in(key, 11), shape, jnp.float32), -6.0, 6.0).astype(jnp.bfloat16)


def raised(values, key, source, target, shards_of, factor):
    owner, partner = [(jnp.arange(values.shape[dim]) // (values.shape[dim] // shards_of)).reshape([-1 if axis == dim else 1 for axis in range(values.ndim)]) for dim in (source, target)]
    chosen = jax.random.permutation(key, shards_of)[partner]
    strong = (owner == chosen) | (owner == (partner + shards_of // 2) % shards_of)
    return jnp.where(strong, factor * values, values)


def steps_of(own_key, shape, shards, smallest, largest):
    loudness, own = 1.0, jax.random.fold_in(own_key, 6)
    for axis_at, parts in shards:
        heights = jnp.exp(jax.random.uniform(jax.random.fold_in(own, axis_at), (parts,), jnp.float32, smallest / len(shards), largest / len(shards)))
        loudness = loudness * jnp.repeat(heights, shape[axis_at] // parts).reshape([-1 if axis == axis_at else 1 for axis in range(len(shape))])
    return loudness


def normal_values(key, dims, width, reach, split=(), kind=jnp.bfloat16):
    array = jax.random.normal(key, dims, jnp.float32) * width
    if len(split) > 0:
        array = steps_of(key, dims, split, -0.22, 0.18) * array
    return jnp.clip(array, min=-reach, max=reach).astype(kind)


def bell_draw_with(stream_key, shape, scale, bound, cuts, heavy, kind=jnp.bfloat16):
    array = scale * jax.random.normal(stream_key, shape, jnp.float32)
    if cuts:
        array = array * steps_of(stream_key, shape, cuts, -0.22, 0.18)
    return jnp.clip(raised(array, jax.random.fold_in(stream_key, 3), *heavy), -bound, bound).astype(kind)


def setup_inputs(seed: int = 0) -> dict:
    splits = jax.random.split(jax.random.key(seed), 7)
    return {
        "patches": normal_values(splits[0], (BATCH, SEQ, P_SIZE), 1.0, 6.0, ((0, 2), (1, 16), (2, 8))),
        "queries": draw_queries(jax.random.fold_in(splits[6], 71), 0),
        "attn_keys": draw_attn_keys(jax.random.fold_in(splits[6], 71), 0),
        "attn_values": normal_values(splits[3], (BATCH, SEQ, HD), 1.0, 6.0, ((0, 2), (1, 16), (2, 8))),
        "out_weight": normal_values(splits[4], (HD, D), (HD // 4) ** -0.5, 0.15625, ((0, 8), (1, 16))),
        "output_grad": bell_draw_with(splits[5], (BATCH, SEQ, D), 0.5, 4.0, ((0, 2), (1, 8), (2, 16)), (2, 1, 16, 2.0)),
    }


def split_heads(tensor):
    shaped = tensor.reshape(BATCH, SEQ, H, DH)
    return jnp.transpose(shaped, (0, 2, 1, 3)).reshape(BATCH * H, SEQ, DH)

def join_heads(tensor):
    shaped = tensor.reshape(BATCH, H, SEQ, DH)
    return jnp.transpose(shaped, (0, 2, 1, 3)).reshape(BATCH, SEQ, H * DH)

def head_probs(query_head, key_head):
    scores = jnp.dot(query_head, key_head.T, preferred_element_type=jnp.float32) * DH ** (-0.5)
    row_max = lax.optimization_barrier(jnp.max(scores, axis=1, keepdims=True))
    log_total = row_max + jnp.log(lax.optimization_barrier(jnp.sum(jnp.exp(scores - row_max), axis=1, keepdims=True)))
    return jnp.exp(scores - log_total).astype(jnp.bfloat16)

def forward_head(operands):
    query_head, key_head, value_head = operands
    attn_probs = head_probs(query_head, key_head)
    return jnp.dot(attn_probs, value_head, preferred_element_type=jnp.float32).astype(jnp.bfloat16)

def backward_head(operands):
    query_head, key_head, value_head, out_head, grad_head = operands
    attn_probs = head_probs(query_head, key_head)
    factor = DH ** (-0.5)
    prob_grad = jnp.dot(grad_head, value_head.T, preferred_element_type=jnp.float32)
    row_dot = lax.optimization_barrier(jnp.sum(grad_head.astype(jnp.float32) * out_head.astype(jnp.float32), axis=1, keepdims=True))
    score_grad = (attn_probs.astype(jnp.float32) * (prob_grad - row_dot)).astype(jnp.bfloat16)
    query_grad = jnp.dot(score_grad, key_head, preferred_element_type=jnp.float32) * factor
    key_grad = jnp.dot(score_grad.T, query_head, preferred_element_type=jnp.float32) * factor
    value_grad = jnp.dot(attn_probs.T, grad_head, preferred_element_type=jnp.float32)
    return (query_grad, key_grad, value_grad)

def attention_grad(flat_grad, out_weight):

    def add_block(running_total, block_index):
        first_col = (block_index * DBLK).astype(jnp.int32)
        grad_cols = lax.dynamic_slice_in_dim(flat_grad, first_col, DBLK, 1)
        weight_cols = lax.dynamic_slice_in_dim(out_weight, first_col, DBLK, 1)
        block_term = jnp.dot(grad_cols, weight_cols.T, preferred_element_type=jnp.float32)
        return (running_total + block_term, None)
    start_total = jnp.zeros((BATCH * SEQ, HD), jnp.float32)
    summed, _ = lax.scan(add_block, start_total, jnp.arange(D // DBLK, dtype=jnp.int32))
    return summed.astype(jnp.bfloat16)

def reference(patches, queries, attn_keys, attn_values, out_weight, output_grad):
    query_heads = split_heads(queries)
    key_heads = split_heads(attn_keys)
    value_heads = split_heads(attn_values)
    out_heads = lax.map(forward_head, (query_heads, key_heads, value_heads))
    attn_out = join_heads(out_heads)
    flat_out = attn_out.reshape(BATCH * SEQ, HD)
    flat_grad = output_grad.reshape(BATCH * SEQ, D)
    flat_patches = patches.reshape(BATCH * SEQ, P_SIZE)
    out_weight_grad = jnp.dot(flat_out.T, flat_grad, preferred_element_type=jnp.float32)
    embed_weight_grad = jnp.dot(flat_patches.T, flat_grad, preferred_element_type=jnp.float32)
    attn_grad = attention_grad(flat_grad, out_weight).reshape(BATCH, SEQ, HD)
    head_grads = lax.map(backward_head, (query_heads, key_heads, value_heads, out_heads, split_heads(attn_grad)))
    return (join_heads(head_grads[0]), join_heads(head_grads[1]), join_heads(head_grads[2]), out_weight_grad, embed_weight_grad)
```

```python
import math

import jax
import jax.numpy as jnp
from jax import lax
from jax.experimental import pallas as pl
from jax.experimental.pallas import tpu as pltpu
from jax.sharding import PartitionSpec as P

DH = 128
MESH = pl.DeviceIdType.MESH
F32 = jnp.float32
BF16 = jnp.bfloat16
FACTOR = DH ** (-0.5)
OWNER_Y = (0, 1, 0, 0, 1, 0)
OWNER_Z = (0, 0, 2, 4, 4, 6)
RS_GAP = 2
AG_GAP = 2
FWD_AT = 6


def plain_dot(left, right):
    return lax.dot_general(left, right, (((1,), (0,)), ((), ())), preferred_element_type=F32)


def dot_t(left, right):
    return lax.dot_general(left, right, (((1,), (1,)), ((), ())), preferred_element_type=F32)


def kernel(
    q_ref, k_ref, v_ref, p_ref, w_ref, g_ref,
    qg_ref, kg_ref, vg_ref, ow_ref, ew_ref,
    gall, wt, qkv, k_t, v_t, rs_in, rs_y, rs_out, d_out, ao, e_buf, s_buf, inv_buf,
    kacc, vacc, og, og_in, ow_out, ow_in, pat, ew_out, ew_in,
    in_s, in_r, g_s, g_r, p_s, p_r, rs_s, rs_r, rsy_r, ag_s, ag_r, ow_s, ow_r, ew_s, ew_r, og_s, og_r,
):
    dp, row, col = lax.axis_index("dp"), lax.axis_index("row"), lax.axis_index("col")
    x, p = lax.div(row, 2), lax.rem(row, 2)
    y, z = lax.div(col, 8), lax.rem(col, 8)

    def mirror(zz):
        return zz * (1 - p) + p * lax.rem(9 - zz, 8)

    zp = mirror(z)
    step_x = 1 - 2 * p

    def at(yy, zz):
        return (dp, row, yy * 8 + mirror(zz))

    def at_x(offset):
        return (dp, lax.rem(x + offset + 4, 4) * 2 + p, col)

    z_up, z_down = lax.rem(zp + 1, 8), lax.rem(zp + 7, 8)
    sibling = (dp, row + 1 - 2 * p, col)
    other_dp = (1 - dp, row, col)
    middle_z = lax.div(lax.rem(zp, 4), 2)
    own_head = 3 * lax.div(zp, 4) + 2 * middle_z + y * (1 - middle_z)
    is_owner = jnp.logical_and(lax.rem(zp, 2) == 0, jnp.logical_or(y == 0, lax.rem(zp, 4) == 0))

    def remote(src, dst, send, recv, device):
        return pltpu.make_async_remote_copy(
            src_ref=src, dst_ref=dst, send_sem=send, recv_sem=recv, device_id=device, device_id_type=MESH
        )

    barrier = pltpu.get_barrier_semaphore()
    for k in range(1, 16):
        pl.semaphore_signal(barrier, inc=1, device_id=(dp, row, lax.rem(col + k, 16)), device_id_type=MESH)
    for device in (at_x(1), at_x(-1), sibling, other_dp):
        pl.semaphore_signal(barrier, inc=1, device_id=device, device_id_type=MESH)
    gall[x, p] = g_ref[...]
    pat[col] = p_ref[...]
    for h in range(6):
        wt[h] = w_ref[h].T
    pl.semaphore_wait(barrier, 19)

    sources = (q_ref, k_ref, v_ref)

    def in_copy(t, h):
        return remote(
            sources[t].at[:, h * DH : (h + 1) * DH], qkv.at[t, col], in_s.at[t, h], in_r.at[t],
            at(OWNER_Y[h], OWNER_Z[h]),
        )

    def owns(h):
        return jnp.logical_and(y == OWNER_Y[h], zp == OWNER_Z[h])

    def g_copy(n, xx, pp, device):
        block = lax.rem(xx + 8, 4)
        return remote(gall.at[block, pp], gall.at[block, pp], g_s.at[n], g_r.at[block, pp], device)

    def g_wait(xx, pp):
        block = lax.rem(xx + 8, 4)
        pltpu.make_async_copy(gall.at[block, pp], gall.at[block, pp], g_r.at[block, pp]).wait()

    g_sends = (
        (0, x, sibling),
        (1, x, at_x(step_x)),
        (2, x, at_x(-step_x)),
        (3, x - step_x, at_x(step_x)),
        (4, x - step_x, sibling),
        (5, x + step_x, sibling),
        (6, x + 2, sibling),
    )

    def g_start(n):
        g_copy(n, g_sends[n][1], p, g_sends[n][2]).start()

    for n in range(3):
        g_start(n)

    for h in range(6):
        @pl.when(owns(h))
        def _():
            for t in range(3):
                pltpu.make_async_copy(
                    sources[t].at[:, h * DH : (h + 1) * DH], qkv.at[t, col], in_r.at[t]
                ).start()

        @pl.when(jnp.logical_not(owns(h)))
        def _():
            for t in range(3):
                in_copy(t, h).start()

    def p_copy(kind, block, device):
        return remote(pat.at[block], pat.at[block], p_s.at[kind, block], p_r.at[block], device)

    def p_wait(block):
        pltpu.make_async_copy(pat.at[block], pat.at[block], p_r.at[block]).wait()

    def block_at(offset):
        return y * 8 + mirror(lax.rem(zp + offset + 8, 8))

    p_copy(0, col, at(y, z_up)).start()
    p_copy(1, col, at(y, z_down)).start()
    p_copy(2, col, at(1 - y, zp)).start()

    def patch_step(k):
        up_block = block_at(-k)
        p_wait(up_block)

        @pl.when(k < 4)
        def _():
            p_copy(0, up_block, at(y, z_up)).start()

        p_copy(2, up_block, at(1 - y, zp)).start()

        @pl.when(k < 4)
        def _():
            down_block = block_at(k)
            p_wait(down_block)

            @pl.when(k < 3)
            def _():
                p_copy(1, down_block, at(y, z_down)).start()

            p_copy(2, down_block, at(1 - y, zp)).start()

    def heads_of(t, j):
        exists = jnp.logical_and(lax.rem(t, 2) == 0, jnp.logical_or(j == 0, lax.rem(t, 4) == 0))
        middle = lax.div(lax.rem(t, 4), 2)
        h = 3 * lax.div(t, 4) + 2 * middle + j * (1 - middle)
        return exists, jnp.minimum(h, 5)

    def owner_y(h):
        return lax.div(lax.rem(h, 3) + 1, 2) * (1 - lax.div(lax.rem(h, 3), 2))

    def partial(h, c):
        return plain_dot(gall[c].reshape(512, 768), wt[h])

    def rs_wait(kind, h, c):
        pltpu.make_async_copy(rs_in.at[kind, h, c], rs_in.at[kind, h, c], rs_r.at[kind, h, c]).wait()

    def rs_chain(i, q):
        c = chunk_of(i)
        dist = 4 - lax.div(q + 1, 2)
        is_min = (1 - lax.rem(q, 2)) * jnp.minimum(q, 1)
        t = lax.rem(zp + is_min * (8 - dist) + (1 - is_min) * dist, 8)
        up = dist + is_min < 4
        nxt = at(y, lax.rem(zp + 1 + 6 * is_min, 8))
        for j in range(2):
            exists, h = heads_of(t, j)

            @pl.when(exists)
            def _():
                total = partial(h, c)

                @pl.when(up)
                def _():
                    rs_wait(is_min, h, c)
                    rs_out[h, c] = (total + rs_in[is_min, h, c].astype(F32)).astype(BF16)

                @pl.when(jnp.logical_not(up))
                def _():
                    rs_out[h, c] = total.astype(BF16)

                remote(
                    rs_out.at[h, c], rs_in.at[is_min, h, c], rs_s.at[h, c], rs_r.at[is_min, h, c], nxt
                ).start()

    def rs_root(i):
        c = chunk_of(i)
        for j in range(2):
            exists, h = heads_of(zp, j)

            @pl.when(jnp.logical_and(exists, owner_y(h) != y))
            def _():
                total = partial(h, c)
                rs_wait(0, h, c)
                rs_wait(1, h, c)
                total = total + rs_in[0, h, c].astype(F32) + rs_in[1, h, c].astype(F32)
                rs_out[h, c] = total.astype(BF16)
                remote(rs_out.at[h, c], rs_y.at[c], rs_s.at[h, c], rsy_r.at[c], at(1 - y, zp)).start()

        @pl.when(is_owner)
        def _():
            total = partial(own_head, c)
            rs_wait(0, own_head, c)
            rs_wait(1, own_head, c)
            total = total + rs_in[0, own_head, c].astype(F32) + rs_in[1, own_head, c].astype(F32)
            pltpu.make_async_copy(rs_y.at[c], rs_y.at[c], rsy_r.at[c]).wait()
            total = total + rs_y[c].astype(F32)
            d_out[c] = total.astype(BF16)

    def chunk_of(i):
        return lax.rem(x + i + lax.div(i, 2) * (1 - 2 * lax.div(i, 3)), 4)

    def fwd_setup():
        for t in range(3):
            pltpu.make_async_copy(qkv.at[t], qkv.at[t], in_r.at[t]).wait()
        for b in range(4):
            k_t[b] = qkv[1, 4 * b : 4 * b + 4].reshape(512, DH).T
            v_t[b] = qkv[2, 4 * b : 4 * b + 4].reshape(512, DH).T

    def queries_of(n):
        return qkv[0, pl.ds(2 * n, 2)].reshape(256, DH)

    def fwd_block(n):
        query = queries_of(n)
        top = None
        for b in range(4):
            s = dot_t(qkv[1, 4 * b : 4 * b + 4].reshape(512, DH), query)
            s_buf[b] = s
            high = jnp.max(s, axis=0, keepdims=True)
            top = high if top is None else jnp.maximum(top, high)
        total, out = None, None
        for b in range(4):
            e = jnp.exp2((s_buf[b] - top) * (FACTOR * math.log2(math.e)))
            part = jnp.sum(e, axis=0, keepdims=True)
            total = part if total is None else total + part
            e = e.astype(BF16)
            e_buf[n, b] = e
            o = plain_dot(v_t[b], e)
            out = o if out is None else out + o
        inv = 1.0 / total
        inv_buf[n] = inv
        ao[own_head, lax.div(n, 2), lax.rem(n, 2)] = (out * inv).astype(BF16)

    def bwd_block(n):
        query = queries_of(n)
        c, half = lax.div(n, 2), lax.rem(n, 2)
        d = d_out[c, pl.ds(pl.multiple_of(half * 256, 256), 256)].astype(F32).T
        d = (d * inv_buf[n]).astype(BF16)
        dot_row = jnp.sum(d.astype(F32) * ao[own_head, c, half].astype(F32), axis=0, keepdims=True)
        grad = None
        for b in range(4):
            rows = slice(4 * b, 4 * b + 4)
            e = e_buf[n, b]
            dprob = plain_dot(qkv[2, rows].reshape(512, DH), d)
            ds = ((dprob - dot_row) * e.astype(F32)).astype(BF16)
            vacc[b] += dot_t(e, d)
            kacc[b] += plain_dot(ds, query)
            part = plain_dot(k_t[b], ds)
            grad = part if grad is None else grad + part
        og[0, pl.ds(2 * n, 2)] = (grad * FACTOR).T.astype(BF16).reshape(2, 128, DH)

    g_wait(x, 1 - p)

    @pl.loop(0, 3 * RS_GAP + 8)
    def _(tau):
        @pl.when(tau == RS_GAP)
        def _():
            g_wait(x - step_x, p)
            g_start(3)
            g_start(4)
            g_wait(x + step_x, p)
            g_start(5)
            g_wait(x - step_x, 1 - p)
            g_wait(x + step_x, 1 - p)

        @pl.when(tau == 3 * RS_GAP)
        def _():
            g_wait(x + 2, p)
            g_start(6)
            g_wait(x + 2, 1 - p)

        @pl.when(jnp.logical_and(tau >= RS_GAP, tau < RS_GAP + 4))
        def _():
            patch_step(tau - RS_GAP + 1)

        @pl.loop(0, 4)
        def _(i):
            q = tau - RS_GAP * i

            @pl.when(jnp.logical_and(q >= 0, q < 7))
            def _():
                rs_chain(i, q)

            @pl.when(q == 7)
            def _():
                rs_root(i)

        @pl.when(jnp.logical_and(is_owner, tau >= FWD_AT))
        def _():
            @pl.when(tau == FWD_AT)
            def _():
                fwd_setup()

            fwd_block(tau - FWD_AT)

    @pl.loop(0, 8)
    def _(k):
        p_wait((1 - y) * 8 + k)

    def ew_add(k, total):
        c, n = lax.div(k, 4), lax.rem(k, 4)
        tokens = gall[c, lax.div(n, 2), pl.ds(pl.multiple_of(lax.rem(n, 2) * 128, 128), 128)]
        return total + plain_dot(pat[k], tokens)

    ew_out[...] = lax.fori_loop(0, 16, ew_add, jnp.zeros((192, 768), F32)).astype(BF16)
    ew_copy = remote(ew_out, ew_in, ew_s, ew_r, other_dp)
    ew_copy.start()

    def ag_copy(kind, h, c, device):
        return remote(ao.at[h, c], ao.at[h, c], ag_s.at[kind, h, c], ag_r.at[h, c], device)

    def ag_wait(h, c):
        pltpu.make_async_copy(ao.at[h, c], ao.at[h, c], ag_r.at[h, c]).wait()

    def ow_copy(h):
        return remote(ow_out.at[h], ow_in.at[h], ow_s.at[h], ow_r.at[h], other_dp)

    def finish_head(h):
        total = None
        for c in range(4):
            for half in range(2):
                part = plain_dot(ao[h, c, half], gall[c, half])
                total = part if total is None else total + part
        ow_out[h] = total.astype(BF16)
        ow_copy(h).start()

    def ag_item(c, q):
        dist = lax.div(q + 1, 2)
        is_min = (1 - lax.rem(q, 2)) * jnp.minimum(q, 1)
        t = lax.rem(zp + is_min * dist + (1 - is_min) * (8 - dist), 8)
        here = q == 0
        for j in range(2):
            exists, h = heads_of(t, j)

            @pl.when(exists)
            def _():
                root = jnp.logical_and(here, owner_y(h) == y)

                @pl.when(jnp.logical_not(root))
                def _():
                    ag_wait(h, c)

                @pl.when(root)
                def _():
                    ag_copy(2, h, c, at(1 - y, zp)).start()

                @pl.when(jnp.logical_and(is_min == 0, dist < 4))
                def _():
                    ag_copy(0, h, c, at(y, z_up)).start()

                @pl.when(jnp.logical_or(here, jnp.logical_and(is_min == 1, dist < 3)))
                def _():
                    ag_copy(1, h, c, at(y, z_down)).start()

                @pl.when(c == 3)
                def _():
                    finish_head(h)

    @pl.when(is_owner)
    def _():
        kacc[...] = jnp.zeros_like(kacc)
        vacc[...] = jnp.zeros_like(vacc)

    @pl.loop(0, 3 * AG_GAP + 8)
    def _(tau):
        @pl.loop(0, 4)
        def _(c):
            q = tau - AG_GAP * c

            @pl.when(jnp.logical_and(q >= 0, q < 8))
            def _():
                ag_item(c, q)

        @pl.when(jnp.logical_and(is_owner, tau < 8))
        def _():
            bwd_block(tau)

    def og_copy(t, k):
        return remote(og.at[t, k], og_in.at[t, own_head], og_s.at[t, k], og_r.at[t], (dp, row, k))

    @pl.when(is_owner)
    def _():
        for b in range(4):
            og[1, 4 * b : 4 * b + 4] = (kacc[b] * FACTOR).astype(BF16).reshape(4, 128, DH)
            og[2, 4 * b : 4 * b + 4] = vacc[b].astype(BF16).reshape(4, 128, DH)

        for t in range(3):
            pltpu.make_async_copy(og.at[t, col], og_in.at[t, own_head], og_r.at[t]).start()

        @pl.loop(1, 16)
        def _(k):
            for t in range(3):
                og_copy(t, lax.rem(col + k, 16)).start()

    ew_copy.wait()
    ew_ref[...] = ew_out[...].astype(F32) + ew_in[...].astype(F32)

    @pl.loop(0, 6)
    def _(h):
        ow_copy(h).wait()
        ow_ref[h] = ow_out[h].astype(F32) + ow_in[h].astype(F32)

    for t, ref in enumerate((qg_ref, kg_ref, vg_ref)):
        pltpu.make_async_copy(og_in.at[t], og_in.at[t], og_r.at[t]).wait()
        for h in range(6):
            ref[:, h * DH : (h + 1) * DH] = og_in[t, h].astype(F32)

    for h in range(6):
        @pl.when(jnp.logical_not(owns(h)))
        def _():
            for t in range(3):
                in_copy(t, h).wait_send()
    for n in range(7):
        g_copy(n, g_sends[n][1], p, g_sends[n][2]).wait_send()

    @pl.loop(0, 8)
    def _(k):
        block = block_at(k)
        p_copy(2, block, at(1 - y, zp)).wait_send()

        @pl.when(jnp.logical_or(k == 0, k > 4))
        def _():
            p_copy(0, block, at(y, z_up)).wait_send()

        @pl.when(k < 3)
        def _():
            p_copy(1, block, at(y, z_down)).wait_send()

    @pl.loop(0, 6)
    def _(h):
        zh = 4 * lax.div(h, 3) + 2 * lax.div(lax.rem(h, 3), 2)
        rel = lax.rem(zp - zh + 8, 8)
        root = jnp.logical_and(rel == 0, owner_y(h) == y)

        @pl.loop(0, 4)
        def _(c):
            @pl.when(jnp.logical_not(root))
            def _():
                pltpu.make_async_copy(rs_out.at[h, c], rs_out.at[h, c], rs_s.at[h, c]).wait()

            @pl.when(root)
            def _():
                ag_copy(2, h, c, at(1 - y, zp)).wait_send()

            @pl.when(rel < 4)
            def _():
                ag_copy(0, h, c, at(y, z_up)).wait_send()

            @pl.when(jnp.logical_or(rel == 0, rel > 5))
            def _():
                ag_copy(1, h, c, at(y, z_down)).wait_send()

    @pl.when(is_owner)
    def _():
        @pl.loop(1, 16)
        def _(k):
            for t in range(3):
                og_copy(t, lax.rem(col + k, 16)).wait_send()


def body(patches, queries, attn_keys, attn_values, out_weight, output_grad):
    patch_t = jnp.pad(patches[0].T, ((0, 10), (0, 0)))
    dma = pltpu.SemaphoreType.DMA
    scratch = [
        pltpu.VMEM((4, 2, 256, 768), BF16),
        pltpu.VMEM((6, 768, DH), BF16),
        pltpu.VMEM((3, 16, 128, DH), BF16),
        pltpu.VMEM((4, DH, 512), BF16),
        pltpu.VMEM((4, DH, 512), BF16),
        pltpu.VMEM((2, 6, 4, 512, DH), BF16),
        pltpu.VMEM((4, 512, DH), BF16),
        pltpu.VMEM((6, 4, 512, DH), BF16),
        pltpu.VMEM((4, 512, DH), BF16),
        pltpu.VMEM((6, 4, 2, DH, 256), BF16),
        pltpu.VMEM((8, 4, 512, 256), BF16),
        pltpu.VMEM((4, 512, 256), F32),
        pltpu.VMEM((8, 1, 256), F32),
        pltpu.VMEM((4, 512, DH), F32),
        pltpu.VMEM((4, 512, DH), F32),
        pltpu.VMEM((3, 16, 128, DH), BF16),
        pltpu.VMEM((3, 6, 128, DH), BF16),
        pltpu.VMEM((6, 128, 768), BF16),
        pltpu.VMEM((6, 128, 768), BF16),
        pltpu.VMEM((16, 192, 128), BF16),
        pltpu.VMEM((192, 768), BF16),
        pltpu.VMEM((192, 768), BF16),
        dma((3, 6)), dma((3,)),
        dma((7,)), dma((4, 2)),
        dma((3, 16)), dma((16,)),
        dma((6, 4)), dma((2, 6, 4)), dma((4,)),
        dma((3, 6, 4)), dma((6, 4)),
        dma((6,)), dma((6,)),
        dma, dma,
        dma((3, 16)), dma((3,)),
    ]
    vmem = pl.BlockSpec(memory_space=pltpu.VMEM)
    qg, kg, vg, ow, ew = pl.pallas_call(
        kernel,
        out_shape=[jax.ShapeDtypeStruct((128, 768), F32)] * 3
        + [jax.ShapeDtypeStruct((6, 128, 768), F32), jax.ShapeDtypeStruct((192, 768), F32)],
        in_specs=[vmem] * 6,
        out_specs=[vmem] * 5,
        scratch_shapes=scratch,
        compiler_params=pltpu.CompilerParams(
            collective_id=0, has_side_effects=True, vmem_limit_bytes=60 * 2**20
        ),
        cost_estimate=pl.CostEstimate(flops=8 * 10**9, bytes_accessed=8 * 10**6, transcendentals=4 * 10**6),
    )(
        queries[0], attn_keys[0], attn_values[0], patch_t,
        out_weight.reshape(6, DH, 768), output_grad[0],
    )
    return (qg[None], kg[None], vg[None], ow.reshape(768, 768), ew[:182])


def solution(mesh):
    placed = (
        P("dp", "col", "row"),
        P("dp", "col", "row"),
        P("dp", "col", "row"),
        P("dp", "col", "row"),
        P("row", "col"),
        P("dp", "row", "col"),
    )
    return jax.shard_map(
        body,
        mesh=mesh,
        in_specs=placed,
        out_specs=(
            P("dp", "col", "row"),
            P("dp", "col", "row"),
            P("dp", "col", "row"),
            P("row", "col"),
            P("row", "col"),
        ),
        check_vma=False,
    )
```

```python
import math

import jax
import jax.numpy as jnp
from jax import lax
from jax.experimental import pallas as pl
from jax.experimental.pallas import tpu as pltpu
from jax.sharding import PartitionSpec as P

DH = 128
MESH = pl.DeviceIdType.MESH
F32 = jnp.float32
BF16 = jnp.bfloat16
FACTOR = DH ** (-0.5)
OWNER_Y = (0, 1, 0, 0, 1, 0)
OWNER_Z = (0, 0, 2, 4, 4, 6)
FWD_AT = 1
AG_AT = 2
BWD_AT = 7
SEND_AT = 11
STEPS = 13


def plain_dot(left, right):
    return lax.dot_general(left, right, (((1,), (0,)), ((), ())), preferred_element_type=F32)


def dot_t(left, right):
    return lax.dot_general(left, right, (((1,), (1,)), ((), ())), preferred_element_type=F32)


def kernel(
    q_ref, k_ref, v_ref, p_ref, w_ref, g_ref,
    qkv_ref, ow_ref, ew_ref,
    gall, wt, qkv, k_t, v_t, rs_in, rs_y, rs_out, d_out, ao, e_buf, s_buf, inv_buf,
    kacc, vacc, ow_acc, og, og_in, ow_out, ow_in, pat, ew_out, ew_in,
    in_s, in_r, g_s, g_r, p_s, p_r, rs_s, rs_r, rsy_r, ag_s, ag_r, ow_s, ow_r, ew_s, ew_r, og_s, og_r,
):
    dp, row, col = lax.axis_index("dp"), lax.axis_index("row"), lax.axis_index("col")
    x, p = lax.div(row, 2), lax.rem(row, 2)
    y, z = lax.div(col, 8), lax.rem(col, 8)

    def mirror(zz):
        return zz * (1 - p) + p * lax.rem(9 - zz, 8)

    zp = mirror(z)
    step_x = 1 - 2 * p

    def at(yy, zz):
        return (dp, row, yy * 8 + mirror(zz))

    def at_x(offset):
        return (dp, lax.rem(x + offset + 4, 4) * 2 + p, col)

    z_up, z_down = lax.rem(zp + 1, 8), lax.rem(zp + 7, 8)
    sibling = (dp, row + 1 - 2 * p, col)
    other_dp = (1 - dp, row, col)
    middle_z = lax.div(lax.rem(zp, 4), 2)
    own_head = 3 * lax.div(zp, 4) + 2 * middle_z + y * (1 - middle_z)
    is_owner = jnp.logical_and(lax.rem(zp, 2) == 0, jnp.logical_or(y == 0, lax.rem(zp, 4) == 0))

    def remote(src, dst, send, recv, device):
        return pltpu.make_async_remote_copy(
            src_ref=src, dst_ref=dst, send_sem=send, recv_sem=recv, device_id=device, device_id_type=MESH
        )

    barrier = pltpu.get_barrier_semaphore()
    for k in range(1, 16):
        pl.semaphore_signal(barrier, inc=1, device_id=(dp, row, lax.rem(col + k, 16)), device_id_type=MESH)
    for device in (at_x(1), at_x(-1), sibling, other_dp):
        pl.semaphore_signal(barrier, inc=1, device_id=device, device_id_type=MESH)
    gall[x, p] = g_ref[...]
    pat[col, 176:192] = jnp.zeros((16, 128), BF16)
    pat[col, 0:182] = p_ref[...]
    for h in range(6):
        wt[h] = w_ref[h].T
    pl.semaphore_wait(barrier, 19)

    sources = (q_ref, k_ref, v_ref)

    def in_copy(t, h):
        return remote(
            sources[t].at[:, h * DH : (h + 1) * DH], qkv.at[t, col], in_s.at[t, h], in_r.at[t],
            at(OWNER_Y[h], OWNER_Z[h]),
        )

    def owns(h):
        return jnp.logical_and(y == OWNER_Y[h], zp == OWNER_Z[h])

    def g_copy(n, xx, pp, device):
        block = lax.rem(xx + 8, 4)
        return remote(gall.at[block, pp], gall.at[block, pp], g_s.at[n], g_r.at[block, pp], device)

    def g_wait(xx, pp):
        block = lax.rem(xx + 8, 4)
        pltpu.make_async_copy(gall.at[block, pp], gall.at[block, pp], g_r.at[block, pp]).wait()

    g_sends = (
        (0, x, sibling),
        (1, x, at_x(step_x)),
        (2, x, at_x(-step_x)),
        (3, x - step_x, at_x(step_x)),
        (4, x - step_x, sibling),
        (5, x + step_x, sibling),
        (6, x + 2, sibling),
    )

    def g_start(n):
        g_copy(n, g_sends[n][1], p, g_sends[n][2]).start()

    for n in range(3):
        g_start(n)

    for h in range(6):
        @pl.when(owns(h))
        def _():
            for t in range(3):
                pltpu.make_async_copy(
                    sources[t].at[:, h * DH : (h + 1) * DH], qkv.at[t, col], in_r.at[t]
                ).start()

        @pl.when(jnp.logical_not(owns(h)))
        def _():
            for t in range(3):
                in_copy(t, h).start()

    def p_copy(kind, block, device):
        return remote(pat.at[block], pat.at[block], p_s.at[kind, block], p_r.at[block], device)

    def p_wait(block):
        pltpu.make_async_copy(pat.at[block], pat.at[block], p_r.at[block]).wait()

    def block_at(offset):
        return y * 8 + mirror(lax.rem(zp + offset + 8, 8))

    p_copy(0, col, at(y, z_up)).start()
    p_copy(1, col, at(y, z_down)).start()
    p_copy(2, col, at(1 - y, zp)).start()

    def patch_step(k):
        up_block = block_at(-k)
        p_wait(up_block)

        @pl.when(k < 4)
        def _():
            p_copy(0, up_block, at(y, z_up)).start()

        p_copy(2, up_block, at(1 - y, zp)).start()

        @pl.when(k < 4)
        def _():
            down_block = block_at(k)
            p_wait(down_block)

            @pl.when(k < 3)
            def _():
                p_copy(1, down_block, at(y, z_down)).start()

            p_copy(2, down_block, at(1 - y, zp)).start()

    def heads_of(t, j):
        exists = jnp.logical_and(lax.rem(t, 2) == 0, jnp.logical_or(j == 0, lax.rem(t, 4) == 0))
        middle = lax.div(lax.rem(t, 4), 2)
        h = 3 * lax.div(t, 4) + 2 * middle + j * (1 - middle)
        return exists, jnp.minimum(h, 5)

    def owner_y(h):
        return lax.div(lax.rem(h, 3) + 1, 2) * (1 - lax.div(lax.rem(h, 3), 2))

    def partial(h, c):
        return plain_dot(gall[c].reshape(512, 768), wt[h])

    def rs_wait(kind, h, c):
        pltpu.make_async_copy(rs_in.at[kind, h, c], rs_in.at[kind, h, c], rs_r.at[kind, h, c]).wait()

    def rs_chain(i, q):
        c = chunk_of(i)
        dist = 4 - lax.div(q + 1, 2)
        is_min = (1 - lax.rem(q, 2)) * jnp.minimum(q, 1)
        t = lax.rem(zp + is_min * (8 - dist) + (1 - is_min) * dist, 8)
        up = dist + is_min < 4
        nxt = at(y, lax.rem(zp + 1 + 6 * is_min, 8))
        for j in range(2):
            exists, h = heads_of(t, j)

            @pl.when(exists)
            def _():
                total = partial(h, c)

                @pl.when(up)
                def _():
                    rs_wait(is_min, h, c)
                    rs_out[h, c] = (total + rs_in[is_min, h, c].astype(F32)).astype(BF16)

                @pl.when(jnp.logical_not(up))
                def _():
                    rs_out[h, c] = total.astype(BF16)

                remote(
                    rs_out.at[h, c], rs_in.at[is_min, h, c], rs_s.at[h, c], rs_r.at[is_min, h, c], nxt
                ).start()

    def rs_root(i):
        c = chunk_of(i)
        for j in range(2):
            exists, h = heads_of(zp, j)

            @pl.when(jnp.logical_and(exists, owner_y(h) != y))
            def _():
                total = partial(h, c)
                rs_wait(0, h, c)
                rs_wait(1, h, c)
                total = total + rs_in[0, h, c].astype(F32) + rs_in[1, h, c].astype(F32)
                rs_out[h, c] = total.astype(BF16)
                remote(rs_out.at[h, c], rs_y.at[c], rs_s.at[h, c], rsy_r.at[c], at(1 - y, zp)).start()

        @pl.when(is_owner)
        def _():
            total = partial(own_head, c)
            rs_wait(0, own_head, c)
            rs_wait(1, own_head, c)
            total = total + rs_in[0, own_head, c].astype(F32) + rs_in[1, own_head, c].astype(F32)
            pltpu.make_async_copy(rs_y.at[c], rs_y.at[c], rsy_r.at[c]).wait()
            total = total + rs_y[c].astype(F32)
            d_out[c] = total.astype(BF16)

    def chunk_of(i):
        return lax.rem(x + i + lax.div(i, 2) * (1 - 2 * lax.div(i, 3)), 4)

    def fwd_setup():
        for t in range(3):
            pltpu.make_async_copy(qkv.at[t], qkv.at[t], in_r.at[t]).wait()
        for b in range(4):
            k_t[b] = qkv[1, 4 * b : 4 * b + 4].reshape(512, DH).T
            v_t[b] = qkv[2, 4 * b : 4 * b + 4].reshape(512, DH).T

    def queries_of(n):
        return qkv[0, pl.ds(2 * n, 2)].reshape(256, DH)

    def fwd_block(n):
        query = queries_of(n)
        top = None
        for b in range(4):
            s = dot_t(qkv[1, 4 * b : 4 * b + 4].reshape(512, DH), query)
            s_buf[b] = s
            high = jnp.max(s, axis=0, keepdims=True)
            top = high if top is None else jnp.maximum(top, high)
        total, out = None, None
        for b in range(4):
            e = jnp.exp2((s_buf[b] - top) * (FACTOR * math.log2(math.e)))
            part = jnp.sum(e, axis=0, keepdims=True)
            total = part if total is None else total + part
            e = e.astype(BF16)
            e_buf[n, b] = e
            o = plain_dot(v_t[b], e)
            out = o if out is None else out + o
        inv = 1.0 / total
        inv_buf[n] = inv
        ao[own_head, lax.div(n, 2), lax.rem(n, 2)] = (out * inv).astype(BF16)

    def og_copy(t, k):
        return remote(og.at[t, k], og_in.at[t, own_head], og_s.at[t, k], og_r.at[t], (dp, row, k))

    def og_send(t, k):
        @pl.when(k == col)
        def _():
            pltpu.make_async_copy(og.at[t, k], og_in.at[t, own_head], og_r.at[t]).start()

        @pl.when(k != col)
        def _():
            og_copy(t, k).start()

    def bwd_block(n):
        query = queries_of(n)
        c, half = lax.div(n, 2), lax.rem(n, 2)
        d = d_out[c, pl.ds(pl.multiple_of(half * 256, 256), 256)].astype(F32).T
        d = (d * inv_buf[n]).astype(BF16)
        dot_row = jnp.sum(d.astype(F32) * ao[own_head, c, half].astype(F32), axis=0, keepdims=True)
        grad = None
        for b in range(4):
            rows = slice(4 * b, 4 * b + 4)
            e = e_buf[n, b]
            dprob = plain_dot(qkv[2, rows].reshape(512, DH), d)
            ds = ((dprob - dot_row) * e.astype(F32)).astype(BF16)
            vacc[b] += dot_t(e, d)
            kacc[b] += plain_dot(ds, query)
            part = plain_dot(k_t[b], ds)
            grad = part if grad is None else grad + part
        og[0, pl.ds(2 * n, 2)] = (grad * FACTOR).T.astype(BF16).reshape(2, 128, DH)
        for k in range(2):
            og_send(0, 2 * n + k)

    def ag_copy(kind, h, c, device):
        return remote(ao.at[h, c], ao.at[h, c], ag_s.at[kind, h, c], ag_r.at[h, c], device)

    def ag_wait(h, c):
        pltpu.make_async_copy(ao.at[h, c], ao.at[h, c], ag_r.at[h, c]).wait()

    def ow_copy(h):
        return remote(ow_out.at[h], ow_in.at[h], ow_s.at[h], ow_r.at[h], other_dp)

    def ow_add(h, i, c):
        part = plain_dot(ao[h, c, 0], gall[c, 0]) + plain_dot(ao[h, c, 1], gall[c, 1])

        @pl.when(i == 0)
        def _():
            ow_acc[h] = part

        @pl.when(jnp.logical_and(i > 0, i < 3))
        def _():
            ow_acc[h] += part

        @pl.when(i == 3)
        def _():
            ow_out[h] = (ow_acc[h] + part).astype(BF16)
            ow_copy(h).start()

    def ag_item(i, q):
        c = chunk_of(i)
        dist = lax.div(q + 1, 2)
        is_min = (1 - lax.rem(q, 2)) * jnp.minimum(q, 1)
        t = lax.rem(zp + is_min * dist + (1 - is_min) * (8 - dist), 8)
        here = q == 0
        for j in range(2):
            exists, h = heads_of(t, j)

            @pl.when(exists)
            def _():
                root = jnp.logical_and(here, owner_y(h) == y)

                @pl.when(jnp.logical_not(root))
                def _():
                    ag_wait(h, c)

                @pl.when(root)
                def _():
                    ag_copy(2, h, c, at(1 - y, zp)).start()

                @pl.when(jnp.logical_and(is_min == 0, dist < 4))
                def _():
                    ag_copy(0, h, c, at(y, z_up)).start()

                @pl.when(jnp.logical_or(here, jnp.logical_and(is_min == 1, dist < 3)))
                def _():
                    ag_copy(1, h, c, at(y, z_down)).start()

                ow_add(h, i, c)

    g_wait(x, 1 - p)

    @pl.when(is_owner)
    def _():
        kacc[...] = jnp.zeros_like(kacc)
        vacc[...] = jnp.zeros_like(vacc)

    @pl.loop(0, STEPS)
    def _(tau):
        @pl.when(tau == 1)
        def _():
            g_wait(x - step_x, p)
            g_start(3)
            g_start(4)
            g_wait(x + step_x, p)
            g_start(5)
            g_wait(x - step_x, 1 - p)
            g_wait(x + step_x, 1 - p)

        @pl.when(tau == 3)
        def _():
            g_wait(x + 2, p)
            g_start(6)
            g_wait(x + 2, 1 - p)

        @pl.loop(0, 4)
        def _(i):
            q = tau - i

            @pl.when(jnp.logical_and(q >= 0, q < 7))
            def _():
                rs_chain(i, q)

            @pl.when(q == 7)
            def _():
                rs_root(i)

        @pl.when(jnp.logical_and(tau >= 2, tau < 6))
        def _():
            patch_step(tau - 1)

        @pl.loop(0, 4)
        def _(i):
            q = tau - AG_AT - i

            @pl.when(jnp.logical_and(q >= 0, q < 8))
            def _():
                ag_item(i, q)

        @pl.when(is_owner)
        def _():
            @pl.when(tau == FWD_AT)
            def _():
                fwd_setup()

            @pl.when(jnp.logical_and(tau >= FWD_AT, tau < FWD_AT + 4))
            def _():
                @pl.loop(0, 2)
                def _(half):
                    fwd_block(2 * chunk_of(tau - FWD_AT) + half)

            @pl.when(jnp.logical_and(tau >= BWD_AT, tau < BWD_AT + 4))
            def _():
                @pl.loop(0, 2)
                def _(half):
                    bwd_block(2 * chunk_of(tau - BWD_AT) + half)

            @pl.when(tau == SEND_AT)
            def _():
                for b in range(4):
                    og[1, 4 * b : 4 * b + 4] = (kacc[b] * FACTOR).astype(BF16).reshape(4, 128, DH)
                    og[2, 4 * b : 4 * b + 4] = vacc[b].astype(BF16).reshape(4, 128, DH)

                @pl.loop(0, 16)
                def _(k):
                    for t in (1, 2):
                        og_send(t, lax.rem(col + k, 16))

    @pl.loop(0, 8)
    def _(k):
        p_wait((1 - y) * 8 + k)

    def ew_add(k, total):
        c, n = lax.div(k, 4), lax.rem(k, 4)
        tokens = gall[c, lax.div(n, 2), pl.ds(pl.multiple_of(lax.rem(n, 2) * 128, 128), 128)]
        return total + plain_dot(pat[k], tokens)

    ew_out[...] = lax.fori_loop(0, 16, ew_add, jnp.zeros((192, 768), F32)).astype(BF16)
    ew_copy = remote(ew_out, ew_in, ew_s, ew_r, other_dp)
    ew_copy.start()

    ew_copy.wait()
    ew_ref[...] = (ew_out[...].astype(F32) + ew_in[...].astype(F32)).astype(BF16)

    @pl.loop(0, 6)
    def _(h):
        ow_copy(h).wait()
        ow_ref[h] = (ow_out[h].astype(F32) + ow_in[h].astype(F32)).astype(BF16)

    for t in range(3):
        pltpu.make_async_copy(og_in.at[t], og_in.at[t], og_r.at[t]).wait()
        for h in range(6):
            qkv_ref[t, :, h * DH : (h + 1) * DH] = og_in[t, h]

    for h in range(6):
        @pl.when(jnp.logical_not(owns(h)))
        def _():
            for t in range(3):
                in_copy(t, h).wait_send()
    for n in range(7):
        g_copy(n, g_sends[n][1], p, g_sends[n][2]).wait_send()

    @pl.loop(0, 8)
    def _(k):
        block = block_at(k)
        p_copy(2, block, at(1 - y, zp)).wait_send()

        @pl.when(jnp.logical_or(k == 0, k > 4))
        def _():
            p_copy(0, block, at(y, z_up)).wait_send()

        @pl.when(k < 3)
        def _():
            p_copy(1, block, at(y, z_down)).wait_send()

    @pl.loop(0, 6)
    def _(h):
        zh = 4 * lax.div(h, 3) + 2 * lax.div(lax.rem(h, 3), 2)
        rel = lax.rem(zp - zh + 8, 8)
        root = jnp.logical_and(rel == 0, owner_y(h) == y)

        @pl.loop(0, 4)
        def _(c):
            @pl.when(jnp.logical_not(root))
            def _():
                pltpu.make_async_copy(rs_out.at[h, c], rs_out.at[h, c], rs_s.at[h, c]).wait()

            @pl.when(root)
            def _():
                ag_copy(2, h, c, at(1 - y, zp)).wait_send()

            @pl.when(rel < 4)
            def _():
                ag_copy(0, h, c, at(y, z_up)).wait_send()

            @pl.when(jnp.logical_or(rel == 0, rel > 5))
            def _():
                ag_copy(1, h, c, at(y, z_down)).wait_send()

    @pl.when(is_owner)
    def _():
        @pl.loop(1, 16)
        def _(k):
            for t in range(3):
                og_copy(t, lax.rem(col + k, 16)).wait_send()


def widen(qkv_ref, ow_ref, ew_ref, qg_ref, kg_ref, vg_ref, ow_out, ew_out):
    for t, ref in enumerate((qg_ref, kg_ref, vg_ref)):
        ref[...] = qkv_ref[t].astype(F32)
    ow_out[...] = ow_ref[...].astype(F32)
    ew_out[...] = ew_ref[0:182].astype(F32)


def body(patches, queries, attn_keys, attn_values, out_weight, output_grad):
    dma = pltpu.SemaphoreType.DMA
    scratch = [
        pltpu.VMEM((4, 2, 256, 768), BF16),
        pltpu.VMEM((6, 768, DH), BF16),
        pltpu.VMEM((3, 16, 128, DH), BF16),
        pltpu.VMEM((4, DH, 512), BF16),
        pltpu.VMEM((4, DH, 512), BF16),
        pltpu.VMEM((2, 6, 4, 512, DH), BF16),
        pltpu.VMEM((4, 512, DH), BF16),
        pltpu.VMEM((6, 4, 512, DH), BF16),
        pltpu.VMEM((4, 512, DH), BF16),
        pltpu.VMEM((6, 4, 2, DH, 256), BF16),
        pltpu.VMEM((8, 4, 512, 256), BF16),
        pltpu.VMEM((4, 512, 256), F32),
        pltpu.VMEM((8, 1, 256), F32),
        pltpu.VMEM((4, 512, DH), F32),
        pltpu.VMEM((4, 512, DH), F32),
        pltpu.VMEM((6, DH, 768), F32),
        pltpu.VMEM((3, 16, 128, DH), BF16),
        pltpu.VMEM((3, 6, 128, DH), BF16),
        pltpu.VMEM((6, 128, 768), BF16),
        pltpu.VMEM((6, 128, 768), BF16),
        pltpu.VMEM((16, 192, 128), BF16),
        pltpu.VMEM((192, 768), BF16),
        pltpu.VMEM((192, 768), BF16),
        dma((3, 6)), dma((3,)),
        dma((7,)), dma((4, 2)),
        dma((3, 16)), dma((16,)),
        dma((6, 4)), dma((2, 6, 4)), dma((4,)),
        dma((3, 6, 4)), dma((6, 4)),
        dma((6,)), dma((6,)),
        dma, dma,
        dma((3, 16)), dma((3,)),
    ]
    vmem = pl.BlockSpec(memory_space=pltpu.VMEM)
    qkv_grad, ow, ew = pl.pallas_call(
        kernel,
        out_shape=[
            jax.ShapeDtypeStruct((3, 128, 768), BF16),
            jax.ShapeDtypeStruct((6, DH, 768), BF16),
            jax.ShapeDtypeStruct((192, 768), BF16),
        ],
        in_specs=[vmem] * 6,
        out_specs=[vmem] * 3,
        scratch_shapes=scratch,
        compiler_params=pltpu.CompilerParams(
            collective_id=0, has_side_effects=True, vmem_limit_bytes=60 * 2**20
        ),
        cost_estimate=pl.CostEstimate(flops=8 * 10**9, bytes_accessed=8 * 10**6, transcendentals=4 * 10**6),
    )(
        queries[0], attn_keys[0], attn_values[0], patches[0].T,
        out_weight.reshape(6, DH, 768), output_grad[0],
    )
    qg, kg, vg, ow, ew = pl.pallas_call(
        widen,
        out_shape=[jax.ShapeDtypeStruct((128, 768), F32)] * 3
        + [jax.ShapeDtypeStruct((768, 768), F32), jax.ShapeDtypeStruct((182, 768), F32)],
        in_specs=[vmem] * 3,
        out_specs=[vmem] * 5,
        compiler_params=pltpu.CompilerParams(vmem_limit_bytes=62 * 2**20),
    )(qkv_grad, ow.reshape(768, 768), ew)
    return (qg[None], kg[None], vg[None], ow, ew)


def solution(mesh):
    placed = (
        P("dp", "col", "row"),
        P("dp", "col", "row"),
        P("dp", "col", "row"),
        P("dp", "col", "row"),
        P("row", "col"),
        P("dp", "row", "col"),
    )
    return jax.shard_map(
        body,
        mesh=mesh,
        in_specs=placed,
        out_specs=(
            P("dp", "col", "row"),
            P("dp", "col", "row"),
            P("dp", "col", "row"),
            P("row", "col"),
            P("row", "col"),
        ),
        check_vma=False,
    )
```

```python
import math

import jax
import jax.numpy as jnp
from jax import lax
from jax.experimental import pallas as pl
from jax.experimental.pallas import tpu as pltpu
from jax.sharding import PartitionSpec as P

DH = 128
MESH = pl.DeviceIdType.MESH
F32 = jnp.float32
BF16 = jnp.bfloat16
FACTOR = DH ** (-0.5)
OWNER_Y = (0, 1, 0, 0, 1, 0)
OWNER_Z = (0, 0, 2, 4, 4, 6)
FWD_AT = 1
AG_AT = 2
BWD_AT = 5
PATCH_AT = 1
EMBED_AT = 5
STEPS = 10
AG_Y = 0


def plain_dot(left, right):
    return lax.dot_general(left, right, (((1,), (0,)), ((), ())), preferred_element_type=F32)


def dot_t(left, right):
    return lax.dot_general(left, right, (((1,), (1,)), ((), ())), preferred_element_type=F32)


def kernel(
    q_ref, k_ref, v_ref, p_ref, w_ref, g_ref,
    qkv_ref, ow_ref, ew_ref,
    gall, wt, qkv, k_t, v_t, rs_in, rs_y, rs_out, d_out, ao, e_buf, s_buf, inv_buf,
    kacc, vacc, ow_acc, og, og_in, ow_out, ow_in, pat, ew_acc, ew_out, ew_in,
    in_s, in_r, g_s, g_r, p_s, p_r, rs_s, rs_r, rsy_r, ag_s, ag_r, ow_s, ow_r, ew_s, ew_r, og_s, og_r,
):
    dp, row, col = lax.axis_index("dp"), lax.axis_index("row"), lax.axis_index("col")
    x, p = lax.div(row, 2), lax.rem(row, 2)
    real_y, z = lax.div(col, 8), lax.rem(col, 8)
    y = real_y * (1 - p) + p * (1 - real_y)

    def mirror(zz):
        return zz * (1 - p) + p * lax.rem(9 - zz, 8)

    zp = mirror(z)
    step_x = 1 - 2 * p

    def at(yy, zz):
        return (dp, row, (yy * (1 - p) + p * (1 - yy)) * 8 + mirror(zz))

    def at_x(offset):
        return (dp, lax.rem(x + offset + 4, 4) * 2 + p, col)

    z_up, z_down = lax.rem(zp + 1, 8), lax.rem(zp + 7, 8)
    sibling = (dp, row + 1 - 2 * p, col)
    other_dp = (1 - dp, row, col)
    middle_z = lax.div(lax.rem(zp, 4), 2)
    own_head = 3 * lax.div(zp, 4) + 2 * middle_z + y * (1 - middle_z)
    is_owner = jnp.logical_and(lax.rem(zp, 2) == 0, jnp.logical_or(y == 0, lax.rem(zp, 4) == 0))

    def remote(src, dst, send, recv, device):
        return pltpu.make_async_remote_copy(
            src_ref=src, dst_ref=dst, send_sem=send, recv_sem=recv, device_id=device, device_id_type=MESH
        )

    barrier = pltpu.get_barrier_semaphore()
    for k in range(1, 16):
        pl.semaphore_signal(barrier, inc=1, device_id=(dp, row, lax.rem(col + k, 16)), device_id_type=MESH)
    for device in (at_x(1), at_x(-1), sibling, other_dp):
        pl.semaphore_signal(barrier, inc=1, device_id=device, device_id_type=MESH)
    gall[x, p] = g_ref[...]
    pat[col, 176:192] = jnp.zeros((16, 128), BF16)
    pat[col, 0:182] = p_ref[...]
    for h in range(6):
        wt[h] = w_ref[h].T
    ow_acc[...] = jnp.zeros_like(ow_acc)
    ew_acc[...] = jnp.zeros_like(ew_acc)
    pl.semaphore_wait(barrier, 19)

    sources = (q_ref, k_ref, v_ref)

    def in_copy(t, h):
        return remote(
            sources[t].at[:, h * DH : (h + 1) * DH], qkv.at[t, col], in_s.at[t, h], in_r.at[t],
            at(OWNER_Y[h], OWNER_Z[h]),
        )

    def owns(h):
        return jnp.logical_and(y == OWNER_Y[h], zp == OWNER_Z[h])

    def g_copy(n, xx, pp, device):
        block = lax.rem(xx + 8, 4)
        return remote(gall.at[block, pp], gall.at[block, pp], g_s.at[n], g_r.at[block, pp], device)

    def g_wait(xx, pp):
        block = lax.rem(xx + 8, 4)
        pltpu.make_async_copy(gall.at[block, pp], gall.at[block, pp], g_r.at[block, pp]).wait()

    g_sends = (
        (0, x, sibling),
        (1, x, at_x(step_x)),
        (2, x, at_x(-step_x)),
        (3, x - step_x, at_x(step_x)),
        (4, x - step_x, sibling),
        (5, x + step_x, sibling),
        (6, x + 2, sibling),
    )

    def g_start(n):
        g_copy(n, g_sends[n][1], p, g_sends[n][2]).start()

    for n in range(3):
        g_start(n)

    for h in range(6):
        @pl.when(owns(h))
        def _():
            for t in range(3):
                pltpu.make_async_copy(
                    sources[t].at[:, h * DH : (h + 1) * DH], qkv.at[t, col], in_r.at[t]
                ).start()

        @pl.when(jnp.logical_not(owns(h)))
        def _():
            for t in range(3):
                in_copy(t, h).start()

    def p_copy(kind, block, device):
        return remote(pat.at[block], pat.at[block], p_s.at[kind, block], p_r.at[block], device)

    def p_wait(block):
        pltpu.make_async_copy(pat.at[block], pat.at[block], p_r.at[block]).wait()

    def block_at(offset):
        return real_y * 8 + mirror(lax.rem(zp + offset + 8, 8))

    p_copy(0, col, at(y, z_up)).start()
    p_copy(1, col, at(y, z_down)).start()
    p_copy(2, col, at(1 - y, zp)).start()

    def patch_step(k):
        up_block = block_at(-k)
        p_wait(up_block)

        @pl.when(k < 4)
        def _():
            p_copy(0, up_block, at(y, z_up)).start()

        p_copy(2, up_block, at(1 - y, zp)).start()

        @pl.when(k < 4)
        def _():
            down_block = block_at(k)
            p_wait(down_block)

            @pl.when(k < 3)
            def _():
                p_copy(1, down_block, at(y, z_down)).start()

            p_copy(2, down_block, at(1 - y, zp)).start()

    def heads_of(t, j):
        exists = jnp.logical_and(lax.rem(t, 2) == 0, jnp.logical_or(j == 0, lax.rem(t, 4) == 0))
        middle = lax.div(lax.rem(t, 4), 2)
        h = 3 * lax.div(t, 4) + 2 * middle + j * (1 - middle)
        return exists, jnp.minimum(h, 5)

    def owner_y(h):
        return lax.div(lax.rem(h, 3) + 1, 2) * (1 - lax.div(lax.rem(h, 3), 2))

    def partial(h, c):
        return plain_dot(gall[c].reshape(512, 768), wt[h])

    def rs_wait(kind, h, c):
        pltpu.make_async_copy(rs_in.at[kind, h, c], rs_in.at[kind, h, c], rs_r.at[kind, h, c]).wait()

    def rs_chain(i, q):
        c = chunk_of(i)
        dist = 4 - lax.div(q + 1, 2)
        is_min = (1 - lax.rem(q, 2)) * jnp.minimum(q, 1)
        t = lax.rem(zp + is_min * (8 - dist) + (1 - is_min) * dist, 8)
        up = dist + is_min < 4
        nxt = at(y, lax.rem(zp + 1 + 6 * is_min, 8))
        for j in range(2):
            exists, h = heads_of(t, j)

            @pl.when(exists)
            def _():
                total = partial(h, c)

                @pl.when(up)
                def _():
                    rs_wait(is_min, h, c)
                    rs_out[h, c] = (total + rs_in[is_min, h, c].astype(F32)).astype(BF16)

                @pl.when(jnp.logical_not(up))
                def _():
                    rs_out[h, c] = total.astype(BF16)

                remote(
                    rs_out.at[h, c], rs_in.at[is_min, h, c], rs_s.at[h, c], rs_r.at[is_min, h, c], nxt
                ).start()

    def rs_cross(i):
        c = chunk_of(i)
        for j in range(2):
            exists, h = heads_of(zp, j)

            @pl.when(jnp.logical_and(exists, owner_y(h) != y))
            def _():
                total = partial(h, c)
                rs_wait(0, h, c)
                rs_wait(1, h, c)
                total = total + rs_in[0, h, c].astype(F32) + rs_in[1, h, c].astype(F32)
                rs_out[h, c] = total.astype(BF16)
                remote(rs_out.at[h, c], rs_y.at[c], rs_s.at[h, c], rsy_r.at[c], at(1 - y, zp)).start()

    def rs_root(i):
        c = chunk_of(i)

        @pl.when(is_owner)
        def _():
            total = partial(own_head, c)
            rs_wait(0, own_head, c)
            rs_wait(1, own_head, c)
            total = total + rs_in[0, own_head, c].astype(F32) + rs_in[1, own_head, c].astype(F32)
            pltpu.make_async_copy(rs_y.at[c], rs_y.at[c], rsy_r.at[c]).wait()
            d_out[c] = (total + rs_y[c].astype(F32)).astype(BF16)

    def chunk_of(i):
        return lax.rem(x + i + lax.div(i, 2) * (1 - 2 * lax.div(i, 3)), 4)

    def fwd_setup():
        for t in range(3):
            pltpu.make_async_copy(qkv.at[t], qkv.at[t], in_r.at[t]).wait()
        for b in range(4):
            k_t[b] = qkv[1, 4 * b : 4 * b + 4].reshape(512, DH).T
            v_t[b] = qkv[2, 4 * b : 4 * b + 4].reshape(512, DH).T

    def queries_of(n):
        return qkv[0, pl.ds(2 * n, 2)].reshape(256, DH)

    def fwd_block(n):
        query = queries_of(n)
        top = None
        for b in range(4):
            s = dot_t(qkv[1, 4 * b : 4 * b + 4].reshape(512, DH), query)
            s_buf[b] = s
            high = jnp.max(s, axis=0, keepdims=True)
            top = high if top is None else jnp.maximum(top, high)
        total, out = None, None
        for b in range(4):
            e = jnp.exp2((s_buf[b] - top) * (FACTOR * math.log2(math.e)))
            part = jnp.sum(e, axis=0, keepdims=True)
            total = part if total is None else total + part
            e = e.astype(BF16)
            e_buf[n, b] = e
            o = plain_dot(v_t[b], e)
            out = o if out is None else out + o
        inv = 1.0 / total
        inv_buf[n] = inv
        ao[own_head, lax.div(n, 2), lax.rem(n, 2)] = (out * inv).astype(BF16)

    def og_copy(t, k):
        return remote(og.at[t, k], og_in.at[t, own_head], og_s.at[t, k], og_r.at[t], (dp, row, k))

    def og_send(t, k):
        @pl.when(k == col)
        def _():
            pltpu.make_async_copy(og.at[t, k], og_in.at[t, own_head], og_r.at[t]).start()

        @pl.when(k != col)
        def _():
            og_copy(t, k).start()

    def bwd_block(n):
        query = queries_of(n)
        c, half = lax.div(n, 2), lax.rem(n, 2)
        d = d_out[c, pl.ds(pl.multiple_of(half * 256, 256), 256)].astype(F32).T
        d = (d * inv_buf[n]).astype(BF16)
        dot_row = jnp.sum(d.astype(F32) * ao[own_head, c, half].astype(F32), axis=0, keepdims=True)
        grad = None
        for b in range(4):
            rows = slice(4 * b, 4 * b + 4)
            e = e_buf[n, b]
            dprob = plain_dot(qkv[2, rows].reshape(512, DH), d)
            ds = ((dprob - dot_row) * e.astype(F32)).astype(BF16)
            vacc[b] += dot_t(e, d)
            kacc[b] += plain_dot(ds, query)
            part = plain_dot(k_t[b], ds)
            grad = part if grad is None else grad + part
        og[0, pl.ds(2 * n, 2)] = (grad * FACTOR).T.astype(BF16).reshape(2, 128, DH)
        for k in range(2):
            og_send(0, 2 * n + k)

    def ag_copy(kind, h, c, device):
        return remote(ao.at[h, c], ao.at[h, c], ag_s.at[kind, h, c], ag_r.at[h, c], device)

    def ag_wait(h, c):
        pltpu.make_async_copy(ao.at[h, c], ao.at[h, c], ag_r.at[h, c]).wait()

    def ow_copy(h):
        return remote(ow_out.at[h], ow_in.at[h], ow_s.at[h], ow_r.at[h], other_dp)

    def ow_add(h, i, c):
        part = plain_dot(ao[h, c, 0], gall[c, 0]) + plain_dot(ao[h, c, 1], gall[c, 1])

        @pl.when(i < 3)
        def _():
            ow_acc[h] += part

        @pl.when(i == 3)
        def _():
            ow_out[h] = (ow_acc[h] + part).astype(BF16)
            ow_copy(h).start()

    def ag_place(q):
        dist = lax.div(q + 1, 2)
        is_min = (1 - lax.rem(q, 2)) * jnp.minimum(q, 1)
        return dist, is_min, lax.rem(zp + is_min * dist + (1 - is_min) * (8 - dist), 8)

    def ag_item(i, q):
        c = chunk_of(i)
        dist, is_min, t = ag_place(q)
        here = q == 0
        for j in range(2):
            exists, h = heads_of(t, j)
            plane = owner_y(h) == y

            @pl.when(jnp.logical_and(exists, jnp.logical_or(i != AG_Y, plane)))
            def _():
                root = jnp.logical_and(here, plane)

                @pl.when(jnp.logical_not(root))
                def _():
                    ag_wait(h, c)

                    @pl.when(jnp.logical_and(is_min == 0, dist < 4))
                    def _():
                        ag_copy(0, h, c, at(y, z_up)).start()

                    @pl.when(jnp.logical_or(here, jnp.logical_and(is_min == 1, dist < 3)))
                    def _():
                        ag_copy(1, h, c, at(y, z_down)).start()

                    @pl.when(i == AG_Y)
                    def _():
                        ag_copy(2, h, c, at(1 - y, zp)).start()

                ow_add(h, i, c)

    def ag_across(q):
        c = chunk_of(AG_Y)
        t = ag_place(q)[2]
        for j in range(2):
            exists, h = heads_of(t, j)

            @pl.when(jnp.logical_and(exists, owner_y(h) != y))
            def _():
                ag_wait(h, c)
                ow_add(h, AG_Y, c)

    ew_copy = remote(ew_out, ew_in, ew_s, ew_r, other_dp)

    def embed_step(c):
        @pl.when(c == 0)
        def _():
            @pl.loop(0, 8)
            def _(k):
                p_wait((1 - real_y) * 8 + k)

        part = None
        for n in range(4):
            tokens = gall[c, n // 2, (n % 2) * 128 : (n % 2) * 128 + 128]
            dot = plain_dot(pat[4 * c + n], tokens)
            part = dot if part is None else part + dot
        ew_acc[...] += part

        @pl.when(c == 3)
        def _():
            ew_out[...] = ew_acc[...].astype(BF16)
            ew_copy.start()

    g_wait(x, 1 - p)

    @pl.when(is_owner)
    def _():
        kacc[...] = jnp.zeros_like(kacc)
        vacc[...] = jnp.zeros_like(vacc)

    def rs_step(tau):
        @pl.loop(0, 4)
        def _(i):
            s = tau - i

            @pl.when(jnp.logical_and(tau == 1, i == 0))
            def _():
                g_wait(x - step_x, p)
                g_start(3)
                g_start(4)

            @pl.when(jnp.logical_and(tau == 1, i == 1))
            def _():
                g_wait(x + step_x, p)
                g_start(5)
                g_wait(x - step_x, 1 - p)
                g_wait(x + step_x, 1 - p)

            @pl.when(jnp.logical_and(tau == 3, i == 3))
            def _():
                g_wait(x + 2, p)
                g_start(6)
                g_wait(x + 2, 1 - p)

            @pl.loop(0, 2)
            def _(m):
                q = 2 * s - 1 + m

                @pl.when(jnp.logical_and(q >= 0, q < 7))
                def _():
                    rs_chain(i, q)

            @pl.when(s == 4)
            def _():
                rs_cross(i)

            @pl.when(s == 5)
            def _():
                rs_root(i)

        @pl.when(jnp.logical_and(tau >= PATCH_AT, tau < PATCH_AT + 4))
        def _():
            patch_step(tau - PATCH_AT + 1)

    def ag_step(tau):
        @pl.loop(0, 2)
        def _(m):
            q = 2 * (tau - AG_AT - AG_Y - 2) - 1 + m

            @pl.when(jnp.logical_and(q >= 0, q < 8))
            def _():
                ag_across(q)

        @pl.loop(0, 4)
        def _(i):
            @pl.loop(0, 2)
            def _(m):
                q = 2 * (tau - AG_AT - i) - 1 + m

                @pl.when(jnp.logical_and(q >= 0, q < 8))
                def _():
                    ag_item(i, q)

    @pl.loop(0, STEPS)
    def _(tau):
        rs_step(tau)
        ag_step(tau)

        @pl.when(jnp.logical_and(tau >= EMBED_AT, tau < EMBED_AT + 4))
        def _():
            embed_step(tau - EMBED_AT)

        @pl.when(is_owner)
        def _():
            @pl.when(tau == FWD_AT)
            def _():
                fwd_setup()

            @pl.when(jnp.logical_and(tau >= FWD_AT, tau < FWD_AT + 4))
            def _():
                @pl.loop(0, 2)
                def _(half):
                    fwd_block(2 * chunk_of(tau - FWD_AT) + half)

                c = chunk_of(tau - FWD_AT)
                ag_copy(2, own_head, c, at(1 - y, zp)).start()
                ag_copy(0, own_head, c, at(y, z_up)).start()
                ag_copy(1, own_head, c, at(y, z_down)).start()

            @pl.when(jnp.logical_and(tau >= BWD_AT, tau < BWD_AT + 4))
            def _():
                @pl.loop(0, 2)
                def _(half):
                    bwd_block(2 * chunk_of(tau - BWD_AT) + half)

            @pl.when(tau == BWD_AT + 3)
            def _():
                for b in range(4):
                    og[1, 4 * b : 4 * b + 4] = (kacc[b] * FACTOR).astype(BF16).reshape(4, 128, DH)
                    og[2, 4 * b : 4 * b + 4] = vacc[b].astype(BF16).reshape(4, 128, DH)

                @pl.loop(0, 16)
                def _(k):
                    for t in (1, 2):
                        og_send(t, lax.rem(col + k, 16))

    ew_copy.wait()
    ew_ref[...] = (ew_out[...].astype(F32) + ew_in[...].astype(F32)).astype(BF16)

    @pl.loop(0, 6)
    def _(h):
        ow_copy(h).wait()
        ow_ref[h] = (ow_out[h].astype(F32) + ow_in[h].astype(F32)).astype(BF16)

    for t in range(3):
        pltpu.make_async_copy(og_in.at[t], og_in.at[t], og_r.at[t]).wait()
        for h in range(6):
            qkv_ref[t, :, h * DH : (h + 1) * DH] = og_in[t, h]

    for h in range(6):
        @pl.when(jnp.logical_not(owns(h)))
        def _():
            for t in range(3):
                in_copy(t, h).wait_send()
    for n in range(7):
        g_copy(n, g_sends[n][1], p, g_sends[n][2]).wait_send()

    @pl.loop(0, 8)
    def _(k):
        block = block_at(k)
        p_copy(2, block, at(1 - y, zp)).wait_send()

        @pl.when(jnp.logical_or(k == 0, k > 4))
        def _():
            p_copy(0, block, at(y, z_up)).wait_send()

        @pl.when(k < 3)
        def _():
            p_copy(1, block, at(y, z_down)).wait_send()

    @pl.loop(0, 6)
    def _(h):
        zh = 4 * lax.div(h, 3) + 2 * lax.div(lax.rem(h, 3), 2)
        rel = lax.rem(zp - zh + 8, 8)
        root = jnp.logical_and(rel == 0, owner_y(h) == y)

        @pl.loop(0, 4)
        def _(c):
            @pl.when(jnp.logical_not(root))
            def _():
                pltpu.make_async_copy(rs_out.at[h, c], rs_out.at[h, c], rs_s.at[h, c]).wait()

            crossing = c == chunk_of(AG_Y)
            plane = owner_y(h) == y
            sends = jnp.logical_or(jnp.logical_not(crossing), plane)

            @pl.when(jnp.logical_or(root, jnp.logical_and(crossing, plane)))
            def _():
                ag_copy(2, h, c, at(1 - y, zp)).wait_send()

            @pl.when(jnp.logical_and(sends, rel < 4))
            def _():
                ag_copy(0, h, c, at(y, z_up)).wait_send()

            @pl.when(jnp.logical_and(sends, jnp.logical_or(rel == 0, rel > 5)))
            def _():
                ag_copy(1, h, c, at(y, z_down)).wait_send()

    @pl.when(is_owner)
    def _():
        @pl.loop(1, 16)
        def _(k):
            for t in range(3):
                og_copy(t, lax.rem(col + k, 16)).wait_send()


def widen(qkv_ref, ow_ref, ew_ref, qg_ref, kg_ref, vg_ref, ow_out, ew_out):
    for t, ref in enumerate((qg_ref, kg_ref, vg_ref)):
        ref[...] = qkv_ref[t].astype(F32)
    ow_out[...] = ow_ref[...].astype(F32)
    ew_out[...] = ew_ref[0:182].astype(F32)


def body(patches, queries, attn_keys, attn_values, out_weight, output_grad):
    dma = pltpu.SemaphoreType.DMA
    scratch = [
        pltpu.VMEM((4, 2, 256, 768), BF16),
        pltpu.VMEM((6, 768, DH), BF16),
        pltpu.VMEM((3, 16, 128, DH), BF16),
        pltpu.VMEM((4, DH, 512), BF16),
        pltpu.VMEM((4, DH, 512), BF16),
        pltpu.VMEM((2, 6, 4, 512, DH), BF16),
        pltpu.VMEM((4, 512, DH), BF16),
        pltpu.VMEM((6, 4, 512, DH), BF16),
        pltpu.VMEM((4, 512, DH), BF16),
        pltpu.VMEM((6, 4, 2, DH, 256), BF16),
        pltpu.VMEM((8, 4, 512, 256), BF16),
        pltpu.VMEM((4, 512, 256), F32),
        pltpu.VMEM((8, 1, 256), F32),
        pltpu.VMEM((4, 512, DH), F32),
        pltpu.VMEM((4, 512, DH), F32),
        pltpu.VMEM((6, DH, 768), F32),
        pltpu.VMEM((3, 16, 128, DH), BF16),
        pltpu.VMEM((3, 6, 128, DH), BF16),
        pltpu.VMEM((6, 128, 768), BF16),
        pltpu.VMEM((6, 128, 768), BF16),
        pltpu.VMEM((16, 192, 128), BF16),
        pltpu.VMEM((192, 768), F32),
        pltpu.VMEM((192, 768), BF16),
        pltpu.VMEM((192, 768), BF16),
        dma((3, 6)), dma((3,)),
        dma((7,)), dma((4, 2)),
        dma((3, 16)), dma((16,)),
        dma((6, 4)), dma((2, 6, 4)), dma((4,)),
        dma((3, 6, 4)), dma((6, 4)),
        dma((6,)), dma((6,)),
        dma, dma,
        dma((3, 16)), dma((3,)),
    ]
    vmem = pl.BlockSpec(memory_space=pltpu.VMEM)
    qkv_grad, ow, ew = pl.pallas_call(
        kernel,
        out_shape=[
            jax.ShapeDtypeStruct((3, 128, 768), BF16),
            jax.ShapeDtypeStruct((6, DH, 768), BF16),
            jax.ShapeDtypeStruct((192, 768), BF16),
        ],
        in_specs=[vmem] * 6,
        out_specs=[vmem] * 3,
        scratch_shapes=scratch,
        compiler_params=pltpu.CompilerParams(
            collective_id=0, has_side_effects=True, vmem_limit_bytes=60 * 2**20
        ),
        cost_estimate=pl.CostEstimate(flops=8 * 10**9, bytes_accessed=8 * 10**6, transcendentals=4 * 10**6),
    )(
        queries[0], attn_keys[0], attn_values[0], patches[0].T,
        out_weight.reshape(6, DH, 768), output_grad[0],
    )
    qg, kg, vg, ow, ew = pl.pallas_call(
        widen,
        out_shape=[jax.ShapeDtypeStruct((128, 768), F32)] * 3
        + [jax.ShapeDtypeStruct((768, 768), F32), jax.ShapeDtypeStruct((182, 768), F32)],
        in_specs=[vmem] * 3,
        out_specs=[vmem] * 5,
        compiler_params=pltpu.CompilerParams(vmem_limit_bytes=62 * 2**20),
    )(qkv_grad, ow.reshape(768, 768), ew)
    return (qg[None], kg[None], vg[None], ow, ew)


def solution(mesh):
    placed = (
        P("dp", "col", "row"),
        P("dp", "col", "row"),
        P("dp", "col", "row"),
        P("dp", "col", "row"),
        P("row", "col"),
        P("dp", "row", "col"),
    )
    return jax.shard_map(
        body,
        mesh=mesh,
        in_specs=placed,
        out_specs=(
            P("dp", "col", "row"),
            P("dp", "col", "row"),
            P("dp", "col", "row"),
            P("row", "col"),
            P("row", "col"),
        ),
        check_vma=False,
    )
```

```python
import math

import jax
import jax.numpy as jnp
from jax import lax
from jax.experimental import pallas as pl
from jax.experimental.pallas import tpu as pltpu
from jax.sharding import PartitionSpec as P

DH = 128
MESH = pl.DeviceIdType.MESH
F32 = jnp.float32
BF16 = jnp.bfloat16
FACTOR = DH ** (-0.5)
OWNER_Y = (0, 1, 0, 0, 1, 0)
OWNER_Z = (0, 0, 2, 4, 4, 6)
FWD_AT = 0
AG_AT = 1
BWD_AT = 5
PATCH_AT = 1
EMBED_AT = 5
STEPS = 9
AG_Y = 0


def plain_dot(left, right):
    return lax.dot_general(left, right, (((1,), (0,)), ((), ())), preferred_element_type=F32)


def dot_t(left, right):
    return lax.dot_general(left, right, (((1,), (1,)), ((), ())), preferred_element_type=F32)


def kernel(
    q_ref, k_ref, v_ref, p_ref, w_ref, g_ref,
    qkv_ref, ow_ref, ew_ref,
    gall, wt, qkv, k_t, v_t, rs_in, rs_y, rs_out, d_out, ao, e_buf, s_buf, inv_buf,
    kacc, vacc, ow_acc, og, og_in, ow_out, ow_in, pat, ew_acc, ew_out, ew_in,
    in_s, in_r, g_s, g_r, p_s, p_r, rs_s, rs_r, rsy_r, ag_s, ag_r, ow_s, ow_r, ew_s, ew_r, og_s, og_r,
):
    dp, row, col = lax.axis_index("dp"), lax.axis_index("row"), lax.axis_index("col")
    x, p = lax.div(row, 2), lax.rem(row, 2)
    real_y, z = lax.div(col, 8), lax.rem(col, 8)
    y = real_y * (1 - p) + p * (1 - real_y)

    def mirror(zz):
        return zz * (1 - p) + p * lax.rem(9 - zz, 8)

    zp = mirror(z)
    step_x = 1 - 2 * p

    def at(yy, zz):
        return (dp, row, (yy * (1 - p) + p * (1 - yy)) * 8 + mirror(zz))

    def at_x(offset):
        return (dp, lax.rem(x + offset + 4, 4) * 2 + p, col)

    z_up, z_down = lax.rem(zp + 1, 8), lax.rem(zp + 7, 8)
    sibling = (dp, row + 1 - 2 * p, col)
    other_dp = (1 - dp, row, col)
    middle_z = lax.div(lax.rem(zp, 4), 2)
    own_head = 3 * lax.div(zp, 4) + 2 * middle_z + y * (1 - middle_z)
    is_owner = jnp.logical_and(lax.rem(zp, 2) == 0, jnp.logical_or(y == 0, lax.rem(zp, 4) == 0))

    def remote(src, dst, send, recv, device):
        return pltpu.make_async_remote_copy(
            src_ref=src, dst_ref=dst, send_sem=send, recv_sem=recv, device_id=device, device_id_type=MESH
        )

    barrier = pltpu.get_barrier_semaphore()
    for k in range(1, 16):
        pl.semaphore_signal(barrier, inc=1, device_id=(dp, row, lax.rem(col + k, 16)), device_id_type=MESH)
    for device in (at_x(1), at_x(-1), sibling, other_dp):
        pl.semaphore_signal(barrier, inc=1, device_id=device, device_id_type=MESH)
    gall[x, p] = g_ref[...]
    pat[col, 176:192] = jnp.zeros((16, 128), BF16)
    pat[col, 0:182] = p_ref[...]
    for h in range(6):
        wt[h] = w_ref[h].T
    ow_acc[...] = jnp.zeros_like(ow_acc)
    ew_acc[...] = jnp.zeros_like(ew_acc)
    pl.semaphore_wait(barrier, 19)

    sources = (q_ref, k_ref, v_ref)

    def in_copy(t, h):
        return remote(
            sources[t].at[:, h * DH : (h + 1) * DH], qkv.at[t, col], in_s.at[t, h], in_r.at[t],
            at(OWNER_Y[h], OWNER_Z[h]),
        )

    def owns(h):
        return jnp.logical_and(y == OWNER_Y[h], zp == OWNER_Z[h])

    def g_copy(n, xx, pp, device):
        block = lax.rem(xx + 8, 4)
        return remote(gall.at[block, pp], gall.at[block, pp], g_s.at[n], g_r.at[block, pp], device)

    def g_wait(xx, pp):
        block = lax.rem(xx + 8, 4)
        pltpu.make_async_copy(gall.at[block, pp], gall.at[block, pp], g_r.at[block, pp]).wait()

    g_sends = (
        (0, x, sibling),
        (1, x, at_x(step_x)),
        (2, x, at_x(-step_x)),
        (3, x - step_x, at_x(step_x)),
        (4, x - step_x, sibling),
        (5, x + step_x, sibling),
        (6, x + 2, sibling),
    )

    def g_start(n):
        g_copy(n, g_sends[n][1], p, g_sends[n][2]).start()

    for n in range(3):
        g_start(n)

    for h in range(6):
        @pl.when(owns(h))
        def _():
            for t in range(3):
                pltpu.make_async_copy(
                    sources[t].at[:, h * DH : (h + 1) * DH], qkv.at[t, col], in_r.at[t]
                ).start()

        @pl.when(jnp.logical_not(owns(h)))
        def _():
            for t in range(3):
                in_copy(t, h).start()

    def p_copy(kind, block, device):
        return remote(pat.at[block], pat.at[block], p_s.at[kind, block], p_r.at[block], device)

    def p_wait(block):
        pltpu.make_async_copy(pat.at[block], pat.at[block], p_r.at[block]).wait()

    def block_at(offset):
        return real_y * 8 + mirror(lax.rem(zp + offset + 8, 8))

    p_copy(0, col, at(y, z_up)).start()
    p_copy(1, col, at(y, z_down)).start()
    p_copy(2, col, at(1 - y, zp)).start()

    def patch_step(k):
        up_block = block_at(-k)
        p_wait(up_block)

        @pl.when(k < 4)
        def _():
            p_copy(0, up_block, at(y, z_up)).start()

        p_copy(2, up_block, at(1 - y, zp)).start()

        @pl.when(k < 4)
        def _():
            down_block = block_at(k)
            p_wait(down_block)

            @pl.when(k < 3)
            def _():
                p_copy(1, down_block, at(y, z_down)).start()

            p_copy(2, down_block, at(1 - y, zp)).start()

    def heads_of(t, j):
        exists = jnp.logical_and(lax.rem(t, 2) == 0, jnp.logical_or(j == 0, lax.rem(t, 4) == 0))
        middle = lax.div(lax.rem(t, 4), 2)
        h = 3 * lax.div(t, 4) + 2 * middle + j * (1 - middle)
        return exists, jnp.minimum(h, 5)

    def owner_y(h):
        return lax.div(lax.rem(h, 3) + 1, 2) * (1 - lax.div(lax.rem(h, 3), 2))

    def partial(h, c):
        return plain_dot(gall[c].reshape(512, 768), wt[h])

    def rs_wait(kind, h, c):
        pltpu.make_async_copy(rs_in.at[kind, h, c], rs_in.at[kind, h, c], rs_r.at[kind, h, c]).wait()

    def rs_chain(i, q):
        c = chunk_of(i)
        dist = 4 - lax.div(q + 1, 2)
        is_min = (1 - lax.rem(q, 2)) * jnp.minimum(q, 1)
        t = lax.rem(zp + is_min * (8 - dist) + (1 - is_min) * dist, 8)
        up = dist + is_min < 4
        nxt = at(y, lax.rem(zp + 1 + 6 * is_min, 8))
        for j in range(2):
            exists, h = heads_of(t, j)

            @pl.when(exists)
            def _():
                total = partial(h, c)

                @pl.when(up)
                def _():
                    rs_wait(is_min, h, c)
                    rs_out[h, c] = (total + rs_in[is_min, h, c].astype(F32)).astype(BF16)

                @pl.when(jnp.logical_not(up))
                def _():
                    rs_out[h, c] = total.astype(BF16)

                remote(
                    rs_out.at[h, c], rs_in.at[is_min, h, c], rs_s.at[h, c], rs_r.at[is_min, h, c], nxt
                ).start()

    def rs_cross(i):
        c = chunk_of(i)
        for j in range(2):
            exists, h = heads_of(zp, j)

            @pl.when(jnp.logical_and(exists, owner_y(h) != y))
            def _():
                total = partial(h, c)
                rs_wait(0, h, c)
                rs_wait(1, h, c)
                total = total + rs_in[0, h, c].astype(F32) + rs_in[1, h, c].astype(F32)
                rs_out[h, c] = total.astype(BF16)
                remote(rs_out.at[h, c], rs_y.at[c], rs_s.at[h, c], rsy_r.at[c], at(1 - y, zp)).start()

    def rs_root(i):
        c = chunk_of(i)

        @pl.when(is_owner)
        def _():
            total = partial(own_head, c)
            rs_wait(0, own_head, c)
            rs_wait(1, own_head, c)
            total = total + rs_in[0, own_head, c].astype(F32) + rs_in[1, own_head, c].astype(F32)
            pltpu.make_async_copy(rs_y.at[c], rs_y.at[c], rsy_r.at[c]).wait()
            d_out[c] = (total + rs_y[c].astype(F32)).astype(BF16)

    def chunk_of(i):
        return lax.rem(x + i + lax.div(i, 2) * (1 - 2 * lax.div(i, 3)), 4)

    def fwd_setup():
        for t in range(3):
            pltpu.make_async_copy(qkv.at[t], qkv.at[t], in_r.at[t]).wait()
        for b in range(4):
            k_t[b] = qkv[1, 4 * b : 4 * b + 4].reshape(512, DH).T
            v_t[b] = qkv[2, 4 * b : 4 * b + 4].reshape(512, DH).T

    def queries_of(n):
        return qkv[0, pl.ds(2 * n, 2)].reshape(256, DH)

    def fwd_block(n):
        query = queries_of(n)
        top = None
        for b in range(4):
            s = dot_t(qkv[1, 4 * b : 4 * b + 4].reshape(512, DH), query)
            s_buf[b] = s
            high = jnp.max(s, axis=0, keepdims=True)
            top = high if top is None else jnp.maximum(top, high)
        total, out = None, None
        for b in range(4):
            e = jnp.exp2((s_buf[b] - top) * (FACTOR * math.log2(math.e)))
            part = jnp.sum(e, axis=0, keepdims=True)
            total = part if total is None else total + part
            e = e.astype(BF16)
            e_buf[n, b] = e
            o = plain_dot(v_t[b], e)
            out = o if out is None else out + o
        inv = 1.0 / total
        inv_buf[n] = inv
        ao[own_head, lax.div(n, 2), lax.rem(n, 2)] = (out * inv).astype(BF16)

    def og_copy(t, k):
        return remote(og.at[t, k], og_in.at[t, own_head], og_s.at[t, k], og_r.at[t], (dp, row, k))

    def og_send(t, k):
        @pl.when(k == col)
        def _():
            pltpu.make_async_copy(og.at[t, k], og_in.at[t, own_head], og_r.at[t]).start()

        @pl.when(k != col)
        def _():
            og_copy(t, k).start()

    def bwd_block(n):
        query = queries_of(n)
        c, half = lax.div(n, 2), lax.rem(n, 2)
        d = d_out[c, pl.ds(pl.multiple_of(half * 256, 256), 256)].astype(F32).T
        d = (d * inv_buf[n]).astype(BF16)
        dot_row = jnp.sum(d.astype(F32) * ao[own_head, c, half].astype(F32), axis=0, keepdims=True)
        grad = None
        for b in range(4):
            rows = slice(4 * b, 4 * b + 4)
            e = e_buf[n, b]
            dprob = plain_dot(qkv[2, rows].reshape(512, DH), d)
            ds = ((dprob - dot_row) * e.astype(F32)).astype(BF16)
            vacc[b] += dot_t(e, d)
            kacc[b] += plain_dot(ds, query)
            part = plain_dot(k_t[b], ds)
            grad = part if grad is None else grad + part
        og[0, pl.ds(2 * n, 2)] = (grad * FACTOR).T.astype(BF16).reshape(2, 128, DH)
        for k in range(2):
            og_send(0, 2 * n + k)

    def ag_copy(kind, h, c, device):
        return remote(ao.at[h, c], ao.at[h, c], ag_s.at[kind, h, c], ag_r.at[h, c], device)

    def ag_wait(h, c):
        pltpu.make_async_copy(ao.at[h, c], ao.at[h, c], ag_r.at[h, c]).wait()

    def ow_copy(h):
        return remote(ow_out.at[h], ow_in.at[h], ow_s.at[h], ow_r.at[h], other_dp)

    def ow_add(h, i, c):
        part = plain_dot(ao[h, c, 0], gall[c, 0]) + plain_dot(ao[h, c, 1], gall[c, 1])

        @pl.when(i < 3)
        def _():
            ow_acc[h] += part

        @pl.when(i == 3)
        def _():
            ow_out[h] = (ow_acc[h] + part).astype(BF16)
            ow_copy(h).start()

    def ag_place(q):
        dist = lax.div(q + 1, 2)
        is_min = (1 - lax.rem(q, 2)) * jnp.minimum(q, 1)
        return dist, is_min, lax.rem(zp + is_min * dist + (1 - is_min) * (8 - dist), 8)

    def ag_item(i, q):
        c = chunk_of(i)
        dist, is_min, t = ag_place(q)
        here = q == 0
        for j in range(2):
            exists, h = heads_of(t, j)
            plane = owner_y(h) == y

            @pl.when(jnp.logical_and(exists, jnp.logical_or(i != AG_Y, plane)))
            def _():
                root = jnp.logical_and(here, plane)

                @pl.when(jnp.logical_not(root))
                def _():
                    ag_wait(h, c)

                    @pl.when(jnp.logical_and(is_min == 0, dist < 4))
                    def _():
                        ag_copy(0, h, c, at(y, z_up)).start()

                    @pl.when(jnp.logical_or(here, jnp.logical_and(is_min == 1, dist < 3)))
                    def _():
                        ag_copy(1, h, c, at(y, z_down)).start()

                    @pl.when(i == AG_Y)
                    def _():
                        ag_copy(2, h, c, at(1 - y, zp)).start()

                ow_add(h, i, c)

    def ag_across(q):
        c = chunk_of(AG_Y)
        t = ag_place(q)[2]
        for j in range(2):
            exists, h = heads_of(t, j)

            @pl.when(jnp.logical_and(exists, owner_y(h) != y))
            def _():
                ag_wait(h, c)
                ow_add(h, AG_Y, c)

    ew_copy = remote(ew_out, ew_in, ew_s, ew_r, other_dp)

    def embed_step(c):
        @pl.when(c == 0)
        def _():
            @pl.loop(0, 8)
            def _(k):
                p_wait((1 - real_y) * 8 + k)

        part = None
        for n in range(4):
            tokens = gall[c, n // 2, (n % 2) * 128 : (n % 2) * 128 + 128]
            dot = plain_dot(pat[4 * c + n], tokens)
            part = dot if part is None else part + dot
        ew_acc[...] += part

        @pl.when(c == 3)
        def _():
            ew_out[...] = ew_acc[...].astype(BF16)
            ew_copy.start()

    g_wait(x, 1 - p)

    @pl.when(is_owner)
    def _():
        kacc[...] = jnp.zeros_like(kacc)
        vacc[...] = jnp.zeros_like(vacc)

    def rs_step(tau):
        @pl.loop(0, 4)
        def _(i):
            s = tau - i

            @pl.when(jnp.logical_and(tau == 0, i == 3))
            def _():
                g_wait(x - step_x, p)
                g_start(3)
                g_start(4)
                g_wait(x + step_x, p)
                g_start(5)

            @pl.when(jnp.logical_and(tau == 1, i == 1))
            def _():
                g_wait(x - step_x, 1 - p)
                g_wait(x + step_x, 1 - p)

            @pl.when(jnp.logical_and(tau == 3, i == 3))
            def _():
                g_wait(x + 2, p)
                g_start(6)
                g_wait(x + 2, 1 - p)

            @pl.loop(0, 2)
            def _(m):
                q = 2 * s - 1 + m

                @pl.when(jnp.logical_and(q >= 0, q < 7))
                def _():
                    rs_chain(i, q)

            @pl.when(s == 4)
            def _():
                rs_cross(i)

            @pl.when(s == 5)
            def _():
                rs_root(i)

        @pl.when(jnp.logical_and(tau >= PATCH_AT, tau < PATCH_AT + 4))
        def _():
            patch_step(tau - PATCH_AT + 1)

    def ag_step(tau):
        @pl.loop(0, 2)
        def _(m):
            q = 2 * (tau - AG_AT - AG_Y - 2) - 1 + m

            @pl.when(jnp.logical_and(q >= 0, q < 8))
            def _():
                ag_across(q)

        @pl.loop(0, 4)
        def _(i):
            @pl.loop(0, 2)
            def _(m):
                q = 2 * (tau - AG_AT - i) - 1 + m

                @pl.when(jnp.logical_and(q >= 0, q < 8))
                def _():
                    ag_item(i, q)

    @pl.loop(0, STEPS)
    def _(tau):
        rs_step(tau)
        ag_step(tau)

        @pl.when(jnp.logical_and(tau >= EMBED_AT, tau < EMBED_AT + 4))
        def _():
            embed_step(tau - EMBED_AT)

        @pl.when(is_owner)
        def _():
            @pl.when(tau == FWD_AT)
            def _():
                fwd_setup()

            @pl.when(jnp.logical_and(tau >= FWD_AT, tau < FWD_AT + 4))
            def _():
                @pl.loop(0, 2)
                def _(half):
                    fwd_block(2 * chunk_of(tau - FWD_AT) + half)

                c = chunk_of(tau - FWD_AT)
                ag_copy(2, own_head, c, at(1 - y, zp)).start()
                ag_copy(0, own_head, c, at(y, z_up)).start()
                ag_copy(1, own_head, c, at(y, z_down)).start()

            @pl.when(jnp.logical_and(tau >= BWD_AT, tau < BWD_AT + 4))
            def _():
                @pl.loop(0, 2)
                def _(half):
                    bwd_block(2 * chunk_of(tau - BWD_AT) + half)

            @pl.when(tau == BWD_AT + 3)
            def _():
                for b in range(4):
                    og[1, 4 * b : 4 * b + 4] = (kacc[b] * FACTOR).astype(BF16).reshape(4, 128, DH)
                    og[2, 4 * b : 4 * b + 4] = vacc[b].astype(BF16).reshape(4, 128, DH)

                @pl.loop(0, 16)
                def _(k):
                    for t in (1, 2):
                        og_send(t, lax.rem(col + k, 16))

    ew_copy.wait()
    ew_ref[...] = (ew_out[...].astype(F32) + ew_in[...].astype(F32)).astype(BF16)

    @pl.loop(0, 6)
    def _(h):
        ow_copy(h).wait()
        ow_ref[h] = (ow_out[h].astype(F32) + ow_in[h].astype(F32)).astype(BF16)

    for t in range(3):
        pltpu.make_async_copy(og_in.at[t], og_in.at[t], og_r.at[t]).wait()
        for h in range(6):
            qkv_ref[t, :, h * DH : (h + 1) * DH] = og_in[t, h]

    for h in range(6):
        @pl.when(jnp.logical_not(owns(h)))
        def _():
            for t in range(3):
                in_copy(t, h).wait_send()
    for n in range(7):
        g_copy(n, g_sends[n][1], p, g_sends[n][2]).wait_send()

    @pl.loop(0, 8)
    def _(k):
        block = block_at(k)
        p_copy(2, block, at(1 - y, zp)).wait_send()

        @pl.when(jnp.logical_or(k == 0, k > 4))
        def _():
            p_copy(0, block, at(y, z_up)).wait_send()

        @pl.when(k < 3)
        def _():
            p_copy(1, block, at(y, z_down)).wait_send()

    @pl.loop(0, 6)
    def _(h):
        zh = 4 * lax.div(h, 3) + 2 * lax.div(lax.rem(h, 3), 2)
        rel = lax.rem(zp - zh + 8, 8)
        root = jnp.logical_and(rel == 0, owner_y(h) == y)

        @pl.loop(0, 4)
        def _(c):
            @pl.when(jnp.logical_not(root))
            def _():
                pltpu.make_async_copy(rs_out.at[h, c], rs_out.at[h, c], rs_s.at[h, c]).wait()

            crossing = c == chunk_of(AG_Y)
            plane = owner_y(h) == y
            sends = jnp.logical_or(jnp.logical_not(crossing), plane)

            @pl.when(jnp.logical_or(root, jnp.logical_and(crossing, plane)))
            def _():
                ag_copy(2, h, c, at(1 - y, zp)).wait_send()

            @pl.when(jnp.logical_and(sends, rel < 4))
            def _():
                ag_copy(0, h, c, at(y, z_up)).wait_send()

            @pl.when(jnp.logical_and(sends, jnp.logical_or(rel == 0, rel > 5)))
            def _():
                ag_copy(1, h, c, at(y, z_down)).wait_send()

    @pl.when(is_owner)
    def _():
        @pl.loop(1, 16)
        def _(k):
            for t in range(3):
                og_copy(t, lax.rem(col + k, 16)).wait_send()


def widen(qkv_ref, ow_ref, ew_ref, qg_ref, kg_ref, vg_ref, ow_out, ew_out):
    for t, ref in enumerate((qg_ref, kg_ref, vg_ref)):
        ref[...] = qkv_ref[t].astype(F32)
    ow_out[...] = ow_ref[...].astype(F32)
    ew_out[...] = ew_ref[0:182].astype(F32)


def body(patches, queries, attn_keys, attn_values, out_weight, output_grad):
    dma = pltpu.SemaphoreType.DMA
    scratch = [
        pltpu.VMEM((4, 2, 256, 768), BF16),
        pltpu.VMEM((6, 768, DH), BF16),
        pltpu.VMEM((3, 16, 128, DH), BF16),
        pltpu.VMEM((4, DH, 512), BF16),
        pltpu.VMEM((4, DH, 512), BF16),
        pltpu.VMEM((2, 6, 4, 512, DH), BF16),
        pltpu.VMEM((4, 512, DH), BF16),
        pltpu.VMEM((6, 4, 512, DH), BF16),
        pltpu.VMEM((4, 512, DH), BF16),
        pltpu.VMEM((6, 4, 2, DH, 256), BF16),
        pltpu.VMEM((8, 4, 512, 256), BF16),
        pltpu.VMEM((4, 512, 256), F32),
        pltpu.VMEM((8, 1, 256), F32),
        pltpu.VMEM((4, 512, DH), F32),
        pltpu.VMEM((4, 512, DH), F32),
        pltpu.VMEM((6, DH, 768), F32),
        pltpu.VMEM((3, 16, 128, DH), BF16),
        pltpu.VMEM((3, 6, 128, DH), BF16),
        pltpu.VMEM((6, 128, 768), BF16),
        pltpu.VMEM((6, 128, 768), BF16),
        pltpu.VMEM((16, 192, 128), BF16),
        pltpu.VMEM((192, 768), F32),
        pltpu.VMEM((192, 768), BF16),
        pltpu.VMEM((192, 768), BF16),
        dma((3, 6)), dma((3,)),
        dma((7,)), dma((4, 2)),
        dma((3, 16)), dma((16,)),
        dma((6, 4)), dma((2, 6, 4)), dma((4,)),
        dma((3, 6, 4)), dma((6, 4)),
        dma((6,)), dma((6,)),
        dma, dma,
        dma((3, 16)), dma((3,)),
    ]
    vmem = pl.BlockSpec(memory_space=pltpu.VMEM)
    qkv_grad, ow, ew = pl.pallas_call(
        kernel,
        out_shape=[
            jax.ShapeDtypeStruct((3, 128, 768), BF16),
            jax.ShapeDtypeStruct((6, DH, 768), BF16),
            jax.ShapeDtypeStruct((192, 768), BF16),
        ],
        in_specs=[vmem] * 6,
        out_specs=[vmem] * 3,
        scratch_shapes=scratch,
        compiler_params=pltpu.CompilerParams(
            collective_id=0, has_side_effects=True, vmem_limit_bytes=60 * 2**20
        ),
        cost_estimate=pl.CostEstimate(flops=8 * 10**9, bytes_accessed=8 * 10**6, transcendentals=4 * 10**6),
    )(
        queries[0], attn_keys[0], attn_values[0], patches[0].T,
        out_weight.reshape(6, DH, 768), output_grad[0],
    )
    qg, kg, vg, ow, ew = pl.pallas_call(
        widen,
        out_shape=[jax.ShapeDtypeStruct((128, 768), F32)] * 3
        + [jax.ShapeDtypeStruct((768, 768), F32), jax.ShapeDtypeStruct((182, 768), F32)],
        in_specs=[vmem] * 3,
        out_specs=[vmem] * 5,
        compiler_params=pltpu.CompilerParams(vmem_limit_bytes=62 * 2**20),
    )(qkv_grad, ow.reshape(768, 768), ew)
    return (qg[None], kg[None], vg[None], ow, ew)


def solution(mesh):
    placed = (
        P("dp", "col", "row"),
        P("dp", "col", "row"),
        P("dp", "col", "row"),
        P("dp", "col", "row"),
        P("row", "col"),
        P("dp", "row", "col"),
    )
    return jax.shard_map(
        body,
        mesh=mesh,
        in_specs=placed,
        out_specs=(
            P("dp", "col", "row"),
            P("dp", "col", "row"),
            P("dp", "col", "row"),
            P("row", "col"),
            P("row", "col"),
        ),
        check_vma=False,
    )
```
